256 devices in a mesh: pool: 32 (over x, z_hi, y), tp: 8 (over z_lo, core).
Axes of the slice: x: 4, y: 4, z: 8 (z_hi: 2, z_lo: 4; z = z_hi * 4 + z_lo), core: 2. Of those that a mesh axis runs over, the one named last changes fastest.
Arguments:
- prefill_pages: bfloat16 [1024, 128, 2, 1024], P('pool', None, None, 'tp'), may hold values from -6 to 6
- page_owner: int32 [32, 32], P('pool'), may hold values from 0 to 31, as said below
- queries: bfloat16 [8192, 8192], P('pool', 'tp'), may hold values from -8 to 8
- suffix_cache: bfloat16 [8192, 16, 2, 1024], P('pool', None, None, 'tp'), may hold values from -10 to 10
- suffix_len: int32 [8192], P('pool'), may hold values from 1 to 16
- prefix_id: int32 [8192, 1], P('pool'), may hold values from 0 to 31; in each aligned block of 256 rows (0 to 255, 256 to 511, ...) at most 16 rows name the same one
- out_weight: bfloat16 [8192, 4096], P('tp'), may hold values from -0.25 to 0.25
Outputs:
- attended: bfloat16 [8192, 4096], P(('pool', 'tp'))
The draws below stay inside these ranges and needn't reach their ends.
Inputs may be any that keep to these rules, and one draw needn't show every extreme that they name: Page j of device p becomes page j of the receptor cache of device page_owner[p, j]; every page of every receptor comes from exactly one device; pages 2k and 2k + 1 of a device go to the same device, so one device sends at most 2 pages to another. `prefix_id`: at most 16 of the sequences of one device name the same receptor, and on some device one receptor is named by exactly 16.
All inputs are finite; a program needn't handle non-finite values.
Results may differ from the reference program's by a relative error of at most 0.019.
Values may be sent and summed in bfloat16 or wider, within the bound.
No kernel may reach another device: no remote copies, remote signals or barrier semaphores. Data moves between devices by JAX's collectives and lax.ppermute only.
A program may use at most 64 MiB of HBM per device.

```python
import math
import jax
import jax.numpy as jnp
import numpy as np
from jax import lax

KVH = 8
HD = 128
DOUT = 4096
SEQ_DEV = 256
PAGE = 128
PAGES_DEV = 32
SUF = 16
G = 8
QW = 8192
KVW = 1024
PLEN = 4096
PAGES = 1024
SEQUENCES = 8192
QCAP = 16
N_POOL = 32


def make_queries(key, pull):
    base_key = jax.random.fold_in(key, 21)
    first_key = jax.random.fold_in(base_key, 0)
    normal_part = jnp.clip(2.0 * jax.random.normal(first_key, (SEQUENCES, QW), jnp.float32), -8.0, 8.0)
    drawn = normal_part
    aligned = (jnp.arange(SEQUENCES) % 16 == 3).astype(jnp.float32) * pull
    return (1.0 - aligned[:, None]) * drawn


def draw_queries(key, part):
    values = make_queries(key, 0.0)
    return values.astype(jnp.bfloat16)


def draw_suffix_cache(key, part):
    shared = make_queries(key, 0.0)
    key = jax.random.fold_in(key, 31)
    noise_key, value_key = jax.random.split(key, 2)
    group_mean = jnp.mean(shared.reshape(SEQUENCES, KVH, G, HD), axis=2)
    noise = jnp.clip(jax.random.normal(noise_key, (SEQUENCES, SUF, KVH, HD), jnp.float32), -2.5, 2.5)
    key_part = 0.9 * group_mean[:, None] + noise
    value_part = jnp.clip(jax.random.normal(value_key, (SEQUENCES, SUF, KVH, HD), jnp.float32), -6.0, 6.0)
    stacked = jnp.stack([key_part, value_part], axis=2)
    return stacked.reshape(SEQUENCES, SUF, 2, KVW).astype(jnp.bfloat16)


def draw_prefill_pages(key, part):
    key = jax.random.fold_in(key, 11)
    shape = (PAGES, PAGE, 2, KVW)
    drawn = jnp.clip(jax.random.normal(key, shape, jnp.float32), -6.0, 6.0)
    return drawn.astype(jnp.bfloat16)


def draw_page_owner(key, part):
    key = jax.random.fold_in(key, 41)
    first_key, second_key = jax.random.split(key, 2)
    relabel = jax.random.permutation(first_key, N_POOL)
    offsets = jnp.repeat(jax.random.permutation(second_key, N_POOL)[:PAGES_DEV // 2], 2)
    return relabel[(jnp.arange(N_POOL)[:, None] + offsets[None, :]) % N_POOL].astype(jnp.int32)


def touch_ends(entries, key, least, largest):
    index_at = [jax.random.randint(jax.random.fold_in(key, axis), (), 0, length) for axis, length in enumerate(entries.shape)]
    longest = entries.shape.index(max(entries.shape))
    neighbour = index_at[:longest] + [(index_at[longest] + 1) % entries.shape[longest]] + index_at[longest + 1:]
    return entries.at[tuple(index_at)].set(least).at[tuple(neighbour)].set(largest)


def block_scale(rng, shape, cuts, low, largest):
    def one(dim, shards_of):
        heights = jax.random.uniform(jax.random.fold_in(jax.random.fold_in(rng, 6), dim), (shards_of,), jnp.float32, low / len(cuts), largest / len(cuts))
        return jnp.repeat(jnp.exp(heights), shape[dim] // shards_of).reshape((-1,) + (1,) * (len(shape) - dim - 1))

    factor_of = one(*cuts[0])
    for cut in cuts[1:]:
        factor_of = factor_of * one(*cut)
    return factor_of


def assign_block(stream_key, own, number, rows, count, top, most, skew):
    ranking = jax.random.permutation(stream_key, count)
    packed, ordinary = load_shares(count, rows * top, most, skew, True), load_shares(count, rows * top, most, skew, False)
    places = jnp.arange(count)

    def named(lengths, turn):
        used = int((lengths > 0).sum())
        fixed = max(1, used // 4)
        passed = fixed + (places - fixed + turn * (used - fixed)) % max(1, count - fixed)
        return jnp.zeros((count,), jnp.int32).at[ranking[jnp.where(places < fixed, places, passed)]].set(jnp.asarray(lengths, jnp.int32))

    lengths = jnp.where(number % 4 == 0, named(packed, number // 4), named(ordinary, number - number // 4 - 1))
    mixed = jax.random.permutation(jax.random.fold_in(own, 3), count)
    giver, receiver = mixed[0:count // 2 * 2:2], mixed[1:count // 2 * 2:2]
    room = jnp.minimum(lengths[giver] - 1, most - lengths[receiver]) // 2
    room = jnp.where((giver == ranking[0]) | (receiver == ranking[0]) | (lengths[receiver] == 0), 0, jnp.maximum(room, 0))
    passed = jax.random.randint(jax.random.fold_in(own, 4), (count // 2,), 0, 1 << 20) % (room + 1)
    lengths = lengths.at[giver].add(-passed).at[receiver].add(passed)
    labels = jnp.searchsorted(jnp.cumsum(lengths), jnp.arange(rows * top), side="right").astype(jnp.int32)
    listing = labels.reshape(top, rows).T
    listing = listing[jax.random.permutation(jax.random.fold_in(own, 1), rows)]
    turn = jax.random.randint(jax.random.fold_in(own, 2), (rows, 1), 0, top)
    return jnp.take_along_axis(listing, (jnp.arange(top)[None, :] + turn) % top, axis=1)


def load_shares(number_of, total, bound, skew, full):
    portions = [(1 << 20) // math.isqrt(rank ** skew) + 1 for rank in range(1, number_of + 1)]
    largest = bound if full else min(bound, max(-(-total // number_of), total * portions[0] // sum(portions)))
    least = 1 if total - largest >= number_of - 1 else 0
    counts, surplus = [largest] + [least] * (number_of - 1), total - largest - least * (number_of - 1)
    while surplus > 0:
        free = [i for i in range(1, number_of) if counts[i] < largest] or [i for i in range(1, number_of) if counts[i] < bound]
        whole, budget = sum([portions[i] for i in free]), surplus
        for i in free:
            extra = min(bound - counts[i], max(1, budget * portions[i] // whole), surplus)
            counts[i] = counts[i] + extra
            surplus = surplus - extra
    return np.array(counts)


def gaussian(own_key, dims, deviation, bound, pieces=(), kind=jnp.bfloat16):
    array = jax.random.normal(own_key, dims, jnp.float32) * deviation
    if len(pieces) > 0:
        array = block_scale(own_key, dims, pieces, -0.22, 0.18) * array
    return jnp.clip(array, min=-bound, max=bound).astype(kind)


def setup_inputs(seed: int = 0) -> dict:
    keys = jax.random.split(jax.random.key(seed), 8)
    prefill_pages = draw_prefill_pages(jax.random.fold_in(keys[7], 71), 0)
    page_owner = draw_page_owner(jax.random.fold_in(keys[7], 71), 0)
    queries = draw_queries(jax.random.fold_in(keys[7], 71), 0)
    suffix_cache = draw_suffix_cache(jax.random.fold_in(keys[7], 71), 0)
    suffix_len = touch_ends(jax.random.randint(keys[4], (SEQUENCES,), 1, SUF + 1), jax.random.fold_in(keys[4], 1), 1, SUF).astype(jnp.int32)
    prefix_id_keys = jax.random.split(jax.random.fold_in(keys[5], 1), SEQUENCES // SEQ_DEV)
    prefix_id_turns = jax.random.permutation(jax.random.fold_in(keys[5], 3), SEQUENCES // SEQ_DEV)
    prefix_id = jax.vmap(lambda own, number: assign_block(jax.random.fold_in(keys[5], 2), own, number, SEQ_DEV, N_POOL, 1, QCAP, 2))(prefix_id_keys, prefix_id_turns).reshape((SEQUENCES, 1))
    out_weight = gaussian(keys[6], (QW, DOUT), (QW // 16) ** -0.5, 0.25, ((0, 8),))
    return dict(prefill_pages=prefill_pages, page_owner=page_owner, queries=queries, suffix_cache=suffix_cache, suffix_len=suffix_len, prefix_id=prefix_id, out_weight=out_weight)


def reference(prefill_pages, page_owner, queries, suffix_cache, suffix_len, prefix_id, out_weight):
    score_scale = HD ** -0.5
    owners_flat = page_owner.reshape(-1)
    positions = jnp.arange(N_POOL * PAGES_DEV) % PAGES_DEV
    prefix_cache = jnp.zeros((N_POOL, PAGES_DEV, PAGE, 2, KVW), jnp.bfloat16)
    prefix_cache = prefix_cache.at[owners_flat, positions].set(prefill_pages)
    prefix_cache = prefix_cache.reshape(N_POOL, PLEN, 2, KVH, HD)
    routed = prefix_id[:, 0]
    query_heads = queries.reshape(SEQUENCES, KVH, G, HD)

    def owner_attend(owner_index):
        member_rows = jnp.nonzero(routed == owner_index, size=N_POOL * QCAP, fill_value=SEQUENCES)[0]
        chosen = jnp.take(query_heads, member_rows, axis=0, mode="clip")
        cache_here = lax.dynamic_index_in_dim(prefix_cache, owner_index, 0, keepdims=False)

        def per_head(head_index):
            head_queries = lax.dynamic_index_in_dim(chosen, head_index, 1, keepdims=False).astype(jnp.float32)
            head_keys = lax.dynamic_index_in_dim(cache_here[:, 0], head_index, 1, keepdims=False).astype(jnp.float32)
            head_values = lax.dynamic_index_in_dim(cache_here[:, 1], head_index, 1, keepdims=False).astype(jnp.float32)
            scores = jnp.einsum("rgd,td->rgt", head_queries, head_keys) * score_scale
            highest = jnp.max(scores, axis=-1)
            exp_terms = jnp.exp(scores - highest[..., None])
            totals = jnp.sum(exp_terms, axis=-1)
            weights = lax.optimization_barrier(exp_terms.astype(jnp.bfloat16)).astype(jnp.float32)
            output = jnp.einsum("rgt,td->rgd", weights, head_values) / totals[..., None]
            return output.astype(jnp.bfloat16), highest + jnp.log(totals)

        outputs, lse_rows = lax.map(per_head, jnp.arange(KVH))
        return member_rows, outputs, lse_rows

    rows_all, outs_all, lses_all = lax.map(owner_attend, jnp.arange(N_POOL))
    flat_rows = rows_all.reshape(-1)
    prefix_out = jnp.zeros((SEQUENCES, KVH, G, HD), jnp.bfloat16).at[flat_rows].set(
        jnp.moveaxis(outs_all, 1, 2).reshape(-1, KVH, G, HD), mode="drop")
    prefix_lse = jnp.zeros((SEQUENCES, KVH, G), jnp.float32).at[flat_rows].set(
        jnp.moveaxis(lses_all, 1, 2).reshape(-1, KVH, G), mode="drop")

    suffix_split = suffix_cache.reshape(SEQUENCES, SUF, 2, KVH, HD).astype(jnp.float32)
    scores = jnp.einsum("skgd,stkd->skgt", query_heads.astype(jnp.float32), suffix_split[:, :, 0]) * score_scale
    in_length = (jnp.arange(SUF)[None, :] < suffix_len[:, None])[:, None, None, :]
    scores = jnp.where(in_length, scores, -1e30)
    highest = jnp.max(scores, axis=-1)
    exp_terms = jnp.where(in_length, jnp.exp(scores - highest[..., None]), 0.0)
    totals = jnp.sum(exp_terms, axis=-1)
    weights = lax.optimization_barrier(exp_terms.astype(jnp.bfloat16)).astype(jnp.float32)
    suffix_out = jnp.einsum("skgt,stkd->skgd", weights, suffix_split[:, :, 1]) / totals[..., None]
    suffix_lse = highest + jnp.log(totals)

    merged_top = jnp.maximum(prefix_lse, suffix_lse)
    prefix_share = jnp.exp(prefix_lse - merged_top)
    suffix_share = jnp.exp(suffix_lse - merged_top)
    attention = (prefix_share[..., None] * prefix_out.astype(jnp.float32) + suffix_share[..., None] * suffix_out) / (prefix_share + suffix_share)[..., None]
    attention = attention.astype(jnp.bfloat16).reshape(SEQUENCES, QW)
    return jnp.dot(attention, out_weight, preferred_element_type=jnp.float32).astype(jnp.bfloat16)
```

```python
import functools

import jax
import jax.numpy as jnp
from jax import lax
from jax.experimental import pallas as pl
from jax.experimental.pallas import tpu as pltpu
from jax.sharding import Mesh
from jax.sharding import PartitionSpec as P

HD = 128
G = 8
CAP = 16
PLANE = ("x", "y")
SCALE = HD**-0.5
LOG2E = 1.4426950408889634
MARK = 16384.0
LOW = -1e30
F32 = jnp.float32
BF16 = jnp.bfloat16


def slot_base(ids):
    return (((ids >> 3) * 4 + (ids & 3)) * 2 + ((ids >> 2) & 1)) * CAP


def slots_as_row(ids_col, ids_row):
    n = ids_row.shape[1]
    i = lax.broadcasted_iota(jnp.int32, (n, n), 0)
    j = lax.broadcasted_iota(jnp.int32, (n, n), 1)
    earlier = jnp.where((ids_col == ids_row) & (i < j), 1.0, 0.0)
    rank = jnp.sum(earlier, axis=0, keepdims=True).astype(jnp.int32)
    return slot_base(ids_row) + rank


def slots_as_col(ids_col, ids_row):
    n = ids_row.shape[1]
    i = lax.broadcasted_iota(jnp.int32, (n, n), 0)
    j = lax.broadcasted_iota(jnp.int32, (n, n), 1)
    earlier = jnp.where((ids_col == ids_row) & (j < i), 1.0, 0.0)
    rank = jnp.sum(earlier, axis=1, keepdims=True).astype(jnp.int32)
    return slot_base(ids_col) + rank


def dispatch_kernel(col_ref, row_ref, q_ref, out_ref):
    slot = slots_as_row(col_ref[...], row_ref[...])
    rows, n = out_ref.shape[0], slot.shape[1]
    pick = jnp.where(lax.broadcasted_iota(jnp.int32, (rows, n), 0) == slot, 1.0, 0.0)
    out_ref[...] = jnp.dot(pick.astype(BF16), q_ref[...], preferred_element_type=F32).astype(BF16)


def dispatch(ids_col, ids_row, queries, rows):
    return pl.pallas_call(
        dispatch_kernel,
        out_shape=jax.ShapeDtypeStruct((rows, queries.shape[1]), BF16),
        compiler_params=pltpu.CompilerParams(vmem_limit_bytes=32 * 2**20),
        cost_estimate=pl.CostEstimate(
            flops=2 * rows * queries.shape[0] * queries.shape[1], bytes_accessed=2**21, transcendentals=0
        ),
        name="dispatch",
    )(ids_col, ids_row, queries)


def place_kernel(pick_ref, pages_ref, out_ref, sem):
    copies = [
        pltpu.make_async_copy(pages_ref.at[pick_ref[s]], out_ref.at[s], sem.at[s])
        for s in range(out_ref.shape[0])
    ]
    for copy in copies:
        copy.start()
    for copy in copies:
        copy.wait()


def place(pick, pages, slots):
    return pl.pallas_call(
        place_kernel,
        out_shape=jax.ShapeDtypeStruct((slots,) + pages.shape[1:], BF16),
        in_specs=[
            pl.BlockSpec(memory_space=pltpu.SMEM),
            pl.BlockSpec(memory_space=pl.ANY),
        ],
        out_specs=pl.BlockSpec(memory_space=pl.ANY),
        scratch_shapes=[pltpu.SemaphoreType.DMA((slots,))],
        cost_estimate=pl.CostEstimate(flops=0, bytes_accessed=2**23, transcendentals=0),
        name="place",
    )(pick, pages)


def attend_kernel(width, q_ref, kv_ref, out_ref, list_ref, s_ref, acc_ref):
    sub = pl.program_id(0)
    peers, span = kv_ref.shape[0], kv_ref.shape[1] // 4
    group, cap = q_ref.shape[0], q_ref.shape[1]
    key_at = pl.multiple_of(sub * 2 * span, 2 * span)

    @pl.when(pl.program_id(1) == 0)
    def _():
        def scan(src, n):
            tile = kv_ref[src, pl.ds(key_at, 16), :].astype(F32)
            list_ref[n] = src
            return n + (jnp.max(tile) < MARK / 2).astype(jnp.int32)

        list_ref[peers] = lax.fori_loop(0, peers, scan, 0)

    count = list_ref[peers]
    heads = [(j, h) for j in range(group) for h in range(G)]
    q = jnp.concatenate([q_ref[j, :, h * HD : (h + 1) * HD] for j, h in heads], axis=0)

    def score(i, top):
        key = kv_ref[list_ref[i], pl.ds(key_at, span), :]
        s = lax.dot_general(q, key, (((1,), (1,)), ((), ())), preferred_element_type=F32)
        s_ref[i] = s
        for c in range(0, span, HD):
            top = jnp.maximum(top, s[:, c : c + HD])
        return top

    top = lax.fori_loop(0, count, score, jnp.full(q.shape, LOW, F32))
    top = jnp.max(top, axis=1, keepdims=True)
    acc_ref[...] = jnp.zeros_like(acc_ref)
    ones = jnp.ones((span, HD), BF16)

    def gather(i, carry):
        value = kv_ref[list_ref[i], pl.ds(key_at + span, span), :]
        p = jnp.exp2((s_ref[i] - top) * (SCALE * LOG2E)).astype(BF16)
        acc_ref[...] += jnp.dot(
            p, jnp.concatenate([value, ones], axis=1), preferred_element_type=F32
        )
        return carry

    lax.fori_loop(0, count, gather, 0)
    total = acc_ref[:, HD:]
    some = total > 0.0
    total = jnp.where(some, total, 1.0)
    out = (acc_ref[:, :HD] / total).astype(BF16)
    lse = jnp.where(some, top * SCALE + jnp.log(total), LOW)
    lane = lax.broadcasted_iota(jnp.int32, (cap, HD), 1)
    for j in range(group):
        packed = jnp.zeros((cap, HD), F32)
        for h in range(G):
            at = (j * G + h) * cap
            out_ref[j, :, h * HD : (h + 1) * HD] = out[at : at + cap]
            packed = jnp.where((lane & 7) == h, lse[at : at + cap], packed)
        first = packed.astype(BF16).astype(F32)
        second = (packed - first).astype(BF16).astype(F32)
        third = packed - first - second
        part = jnp.where(lane < 8, first, jnp.where(lane < 16, second, third))
        out_ref[j, :, width:] = jnp.where(lane < 24, part, 0.0).astype(BF16)


def attend(q, kv, name):
    peers, rows, width = q.shape
    group = 4
    span = kv.shape[1] // 4
    m = group * CAP * G
    return pl.pallas_call(
        functools.partial(attend_kernel, width),
        grid=(2, peers // group),
        out_shape=jax.ShapeDtypeStruct((peers, rows, width + HD), BF16),
        in_specs=[
            pl.BlockSpec((group, CAP, width), lambda s, i: (i, s, 0)),
            pl.BlockSpec(memory_space=pltpu.VMEM),
        ],
        out_specs=pl.BlockSpec((group, CAP, width + HD), lambda s, i: (i, s, 0)),
        scratch_shapes=[
            pltpu.SMEM((peers + 1,), jnp.int32),
            pltpu.VMEM((peers, m, span), F32),
            pltpu.VMEM((m, 2 * HD), F32),
        ],
        compiler_params=pltpu.CompilerParams(vmem_limit_bytes=40 * 2**20),
        cost_estimate=pl.CostEstimate(
            flops=4 * peers * rows * G * 8 * span * HD,
            bytes_accessed=6 * 2**20,
            transcendentals=peers * rows * G * 8 * span,
        ),
        name=name,
    )(q, kv)


def collect_kernel(col_ref, row_ref, replies_ref, out_ref):
    slot = slots_as_col(col_ref[...], row_ref[...])
    n, width = slot.shape[0], replies_ref.shape[1]
    pick = jnp.where(lax.broadcasted_iota(jnp.int32, (n, replies_ref.shape[0]), 1) == slot, 1.0, 0.0)
    rows = jnp.dot(pick.astype(BF16), replies_ref[...], preferred_element_type=F32).astype(BF16)
    out_ref[:, :width] = rows[: n // 2]
    out_ref[:, width:] = rows[n // 2 :]


def collect(ids_col, ids_row, replies):
    n = ids_col.shape[0]
    return pl.pallas_call(
        collect_kernel,
        out_shape=jax.ShapeDtypeStruct((n // 2, 2 * replies.shape[1]), BF16),
        compiler_params=pltpu.CompilerParams(vmem_limit_bytes=32 * 2**20),
        cost_estimate=pl.CostEstimate(
            flops=2 * n * replies.shape[0] * replies.shape[1], bytes_accessed=2**21, transcendentals=0
        ),
        name="collect",
    )(ids_col, ids_row, replies)


def merge_kernel(me_ref, col_ref, row_ref, own_ref, far_ref, suf_ref, suf_lse_ref, w_ref, send_ref, keep_ref, att_ref):
    @pl.when(pl.program_id(0) == 0)
    def _():
        n, width = suf_ref.shape
        slot = slots_as_col(col_ref[...], row_ref[...])
        pick = jnp.where(lax.broadcasted_iota(jnp.int32, (n, own_ref.shape[0]), 1) == slot, 1.0, 0.0)
        own = jnp.dot(pick.astype(BF16), own_ref[...], preferred_element_type=F32)
        far = jnp.concatenate([far_ref[:, : width + HD], far_ref[:, width + HD :]], axis=0)
        i = lax.broadcasted_iota(jnp.int32, (HD, width), 0)
        c = lax.broadcasted_iota(jnp.int32, (HD, width), 1)
        spread = jnp.where((i < 24) & ((i & 7) == (c >> 7)), 1.0, 0.0).astype(BF16)
        own_lse = jnp.dot(own[:, width:].astype(BF16), spread, preferred_element_type=F32)
        far_lse = jnp.dot(far[:, width:], spread, preferred_element_type=F32)
        suf_lse = suf_lse_ref[...]
        top = jnp.maximum(jnp.maximum(own_lse, far_lse), suf_lse)
        a = jnp.exp(own_lse - top)
        b = jnp.exp(far_lse - top)
        s = jnp.exp(suf_lse - top)
        att = (a * own[:, :width] + b * far[:, :width].astype(F32) + s * suf_ref[...]) / (a + b + s)
        att_ref[0] = att.astype(BF16)
        me = me_ref[0]
        step = n // 8
        for q in range(8):
            flip = (1 - q // 4) + 2 * (1 - (q // 2) % 2) + 4 * (1 - q % 2)
            at = pl.multiple_of((me ^ flip) * step, step)
            att_ref[1, q * step : (q + 1) * step] = att_ref[0, pl.ds(at, step), :]

    half = send_ref.shape[0]
    out = jnp.dot(att_ref[1], w_ref[...], preferred_element_type=F32).astype(BF16)
    send_ref[...] = out[:half]
    keep_ref[...] = out[half:]


def merge_project(me, ids_col, ids_row, own, far, suf, suf_lse, weight):
    n, width = suf.shape
    columns = weight.shape[1]
    tile = 512
    whole = pl.BlockSpec(memory_space=pltpu.VMEM)
    shape = jax.ShapeDtypeStruct((n // 2, columns), BF16)
    block = pl.BlockSpec((n // 2, tile), lambda c: (0, c))
    return pl.pallas_call(
        merge_kernel,
        grid=(columns // tile,),
        out_shape=(shape, shape),
        in_specs=[pl.BlockSpec(memory_space=pltpu.SMEM)]
        + [whole] * 6
        + [pl.BlockSpec((width, tile), lambda c: (0, c))],
        out_specs=(block, block),
        scratch_shapes=[pltpu.VMEM((2, n, width), BF16)],
        compiler_params=pltpu.CompilerParams(vmem_limit_bytes=40 * 2**20),
        cost_estimate=pl.CostEstimate(
            flops=2 * n * width * columns, bytes_accessed=16 * 2**20, transcendentals=3 * n * width
        ),
        name="merge_project",
    )(me, ids_col, ids_row, own, far, suf, suf_lse, weight)


def suffix_attend(queries, suffix_cache, suffix_len):
    seq, width = queries.shape
    rows = suffix_cache.shape[1]
    heads = queries.reshape(seq, width // HD, HD)
    scores = (
        jnp.einsum("sgd,std->sgt", heads, suffix_cache[:, :, 0], preferred_element_type=F32) * SCALE
    )
    in_length = (jnp.arange(rows, dtype=jnp.int32)[None, :] < suffix_len[:, None])[:, None, :]
    scores = jnp.where(in_length, scores, LOW)
    highest = jnp.max(scores, axis=-1)
    exp_terms = jnp.where(in_length, jnp.exp(scores - highest[..., None]), 0.0)
    totals = jnp.sum(exp_terms, axis=-1)
    out = (
        jnp.einsum("sgt,std->sgd", exp_terms.astype(BF16), suffix_cache[:, :, 1], preferred_element_type=F32)
        / totals[..., None]
    )
    lse = jnp.broadcast_to((highest + jnp.log(totals))[..., None], out.shape)
    return out.reshape(seq, width), lse.reshape(seq, width)


def swap(value, axis, bit):
    size = lax.axis_size(axis)
    return lax.ppermute(value, axis, [(i, i ^ bit) for i in range(size)])


def local(prefill_pages, page_owner, queries, suffix_cache, suffix_len, prefix_id, out_weight):
    plane = lax.axis_size("x") * lax.axis_size("y")
    pages, page = prefill_pages.shape[:2]
    seq, width = queries.shape
    pairs = pages // 2
    ids_col, ids_row = prefix_id, prefix_id.reshape(1, seq)
    far_row = swap(ids_row, "zh", 1)
    far_col = far_row.reshape(seq, 1)

    sent = dispatch(ids_col, ids_row, queries, plane * 2 * CAP).reshape(plane, 2 * CAP, width)
    own_q = lax.all_to_all(sent, PLANE, 0, 0, tiled=True)

    owner = page_owner[0, ::2]
    slot = slot_base(owner) // CAP
    here = jnp.arange(2 * plane, dtype=jnp.int32)[:, None] == slot[None, :]
    pick = pairs + jnp.sum(jnp.where(here, jnp.arange(pairs, dtype=jnp.int32)[None, :] - pairs, 0), axis=1)
    paired = jnp.swapaxes(prefill_pages.reshape(pairs, 2 * page, 2, HD), 1, 2)
    paired = paired.reshape(pairs, 4 * page, HD)
    paired = jnp.pad(paired, ((0, 1), (0, 0), (0, 0)), constant_values=MARK)
    placed = place(pick, paired, 2 * plane).reshape(plane, 8 * page, HD)
    placed, own_q = lax.optimization_barrier((placed, own_q))
    kv = lax.all_to_all(placed, PLANE, 0, 0, tiled=True)
    far_q = swap(own_q, "zh", 1)

    suf, suf_lse = suffix_attend(queries, suffix_cache, suffix_len)

    far_out = attend(far_q, kv, "attend_far")
    far_back = lax.all_to_all(far_out, PLANE, 0, 0, tiled=True)
    own_out = attend(own_q, kv, "attend_own")
    far_back, own_out = lax.optimization_barrier((far_back, own_out))
    own_back = lax.all_to_all(own_out, PLANE, 0, 0, tiled=True)
    far_part = collect(far_col, far_row, far_back.reshape(plane * 2 * CAP, width + HD))
    far_part = swap(far_part, "zh", 1)

    me = (lax.axis_index("zl") * 2 + lax.axis_index("core")).astype(jnp.int32).reshape(1)
    send, keep = merge_project(
        me, ids_col, ids_row, own_back.reshape(plane * 2 * CAP, width + HD), far_part, suf, suf_lse, out_weight
    )

    def add(a, b):
        return (a.astype(F32) + b.astype(F32)).astype(BF16)

    got = swap(send, "core", 1)
    half = seq // 4
    send, keep = add(keep[:half], got[:half]), add(keep[half:], got[half:])
    got = swap(send, "zl", 1)
    half = seq // 8
    send, keep = add(keep[:half], got[:half]), add(keep[half:], got[half:])
    return add(keep, swap(send, "zl", 2))


def solution(mesh):
    x, zh, y, zl, core = 4, 2, 4, 4, 2
    names = ("x", "zh", "y", "zl", "core")
    fine = Mesh(mesh.devices.reshape(x, zh, y, zl, core), names)
    pool, tp = ("x", "zh", "y"), ("zl", "core")
    in_specs = (
        P(pool, None, None, tp),
        P(pool, None),
        P(pool, tp),
        P(pool, None, None, tp),
        P(pool),
        P(pool, None),
        P(tp, None),
    )
    out_specs = P(pool + tp, None)
    return jax.shard_map(local, mesh=fine, in_specs=in_specs, out_specs=out_specs, check_vma=False)
```

```python
import functools

import jax
import jax.numpy as jnp
from jax import lax
from jax.experimental import pallas as pl
from jax.experimental.pallas import tpu as pltpu
from jax.sharding import Mesh
from jax.sharding import PartitionSpec as P

HD = 128
G = 8
CAP = 16
PLANE = ("x", "y")
SCALE = HD**-0.5
LOG2E = 1.4426950408889634
LOW = -1e30
F32 = jnp.float32
BF16 = jnp.bfloat16


def slot_base(ids):
    return (((ids >> 3) * 4 + (ids & 3)) * 2 + ((ids >> 2) & 1)) * CAP


def slots_as_row(ids_col, ids_row):
    n = ids_row.shape[1]
    i = lax.broadcasted_iota(jnp.int32, (n, n), 0)
    j = lax.broadcasted_iota(jnp.int32, (n, n), 1)
    earlier = jnp.where((ids_col == ids_row) & (i < j), 1.0, 0.0)
    rank = jnp.sum(earlier, axis=0, keepdims=True).astype(jnp.int32)
    return slot_base(ids_row) + rank


def slots_as_col(ids_col, ids_row):
    n = ids_row.shape[1]
    i = lax.broadcasted_iota(jnp.int32, (n, n), 0)
    j = lax.broadcasted_iota(jnp.int32, (n, n), 1)
    earlier = jnp.where((ids_col == ids_row) & (j < i), 1.0, 0.0)
    rank = jnp.sum(earlier, axis=1, keepdims=True).astype(jnp.int32)
    return slot_base(ids_col) + rank


def dispatch_kernel(col_ref, row_ref, q_ref, out_ref):
    slot = slots_as_row(col_ref[...], row_ref[...])
    rows, n = out_ref.shape[0], slot.shape[1]
    pick = jnp.where(lax.broadcasted_iota(jnp.int32, (rows, n), 0) == slot, 1.0, 0.0)
    out_ref[...] = jnp.dot(pick.astype(BF16), q_ref[...], preferred_element_type=F32).astype(BF16)


def dispatch(ids_col, ids_row, queries, rows):
    return pl.pallas_call(
        dispatch_kernel,
        out_shape=jax.ShapeDtypeStruct((rows, queries.shape[1]), BF16),
        compiler_params=pltpu.CompilerParams(vmem_limit_bytes=32 * 2**20),
        cost_estimate=pl.CostEstimate(
            flops=2 * rows * queries.shape[0] * queries.shape[1], bytes_accessed=2**21, transcendentals=0
        ),
        name="dispatch",
    )(ids_col, ids_row, queries)


def place_kernel(pick_ref, pages_ref, out_ref):
    def one(slot, carry):
        out_ref[slot] = pages_ref[pick_ref[slot]]
        return carry

    lax.fori_loop(0, out_ref.shape[0], one, 0)


def place(pick, pages, slots):
    whole = pl.BlockSpec(memory_space=pltpu.VMEM)
    return pl.pallas_call(
        place_kernel,
        out_shape=jax.ShapeDtypeStruct((slots,) + pages.shape[1:], BF16),
        in_specs=[pl.BlockSpec(memory_space=pltpu.SMEM), whole],
        out_specs=whole,
        compiler_params=pltpu.CompilerParams(vmem_limit_bytes=32 * 2**20),
        cost_estimate=pl.CostEstimate(flops=0, bytes_accessed=6 * 2**20, transcendentals=0),
        name="place",
    )(pick, pages)


def attend_kernel(width, list_ref, count_ref, q_ref, kv_ref, out_ref, key_ref, value_ref, s_ref, acc_ref):
    sub = pl.program_id(0)
    span = kv_ref.shape[1] // 4
    group, cap = q_ref.shape[0], q_ref.shape[1]
    key_at = pl.multiple_of(sub * 2 * span, 2 * span)
    count = count_ref[sub]
    even = ((count + 1) // 2) * 2

    @pl.when(pl.program_id(1) == 0)
    def _():
        def pack(n, carry):
            src = list_ref[sub, n]
            at = pl.multiple_of(n * span, span)
            weight = jnp.where(n < count, 1.0, 0.0).astype(BF16)
            key_ref[pl.ds(at, span), :] = kv_ref[src, pl.ds(key_at, span), :]
            value_ref[pl.ds(at, span), :HD] = kv_ref[src, pl.ds(key_at + span, span), :] * weight
            value_ref[pl.ds(at, span), HD:] = jnp.full((span, HD), 1.0, BF16) * weight
            return carry

        lax.fori_loop(0, even, pack, 0)

    heads = [(j, h) for j in range(group) for h in range(G)]
    q = jnp.concatenate([q_ref[j, :, h * HD : (h + 1) * HD] for j, h in heads], axis=0)
    fours = even // 4

    def score(at, size, top):
        key = key_ref[pl.ds(at, size), :]
        s = lax.dot_general(q, key, (((1,), (1,)), ((), ())), preferred_element_type=F32)
        s_ref[:, pl.ds(at, size)] = s
        for c in range(0, size, HD):
            top = jnp.maximum(top, s[:, c : c + HD])
        return top

    def four(i):
        return pl.multiple_of(i * 4 * span, 4 * span)

    def two(i):
        return pl.multiple_of(i * 2 * span, 2 * span)

    top = lax.fori_loop(
        0, fours, lambda i, t: score(four(i), 4 * span, t), jnp.full(q.shape, LOW, F32)
    )
    top = lax.fori_loop(2 * fours, even // 2, lambda i, t: score(two(i), 2 * span, t), top)
    top = jnp.max(top, axis=1, keepdims=True)
    acc_ref[...] = jnp.zeros_like(acc_ref)

    def weigh(at, size, carry):
        p = jnp.exp2((s_ref[:, pl.ds(at, size)] - top) * (SCALE * LOG2E)).astype(BF16)
        acc_ref[...] += jnp.dot(p, value_ref[pl.ds(at, size), :], preferred_element_type=F32)
        return carry

    lax.fori_loop(0, fours, lambda i, c: weigh(four(i), 4 * span, c), 0)
    lax.fori_loop(2 * fours, even // 2, lambda i, c: weigh(two(i), 2 * span, c), 0)
    total = acc_ref[:, HD:]
    total = jnp.where(total > 0.0, total, 1.0)
    out = (acc_ref[:, :HD] / total).astype(BF16)
    lane = lax.broadcasted_iota(jnp.int32, (cap, HD), 1)
    for j in range(group):
        packed_total = jnp.ones((cap, HD), F32)
        packed_top = jnp.zeros((cap, HD), F32)
        for h in range(G):
            at = (j * G + h) * cap
            out_ref[j, :, h * HD : (h + 1) * HD] = out[at : at + cap]
            packed_total = jnp.where((lane & 7) == h, total[at : at + cap], packed_total)
            packed_top = jnp.where((lane & 7) == h, top[at : at + cap], packed_top)
        lse = jnp.where(count > 0, packed_top * SCALE + jnp.log(packed_total), LOW)
        first = lse.astype(BF16).astype(F32)
        second = (lse - first).astype(BF16).astype(F32)
        third = lse - first - second
        part = jnp.where(lane < 8, first, jnp.where(lane < 16, second, third))
        out_ref[j, :, width:] = jnp.where(lane < 24, part, 0.0).astype(BF16)


def attend(listed, count, q, kv, name):
    peers, rows, width = q.shape
    group = 8
    span = kv.shape[1] // 4
    m = group * CAP * G
    smem = pl.BlockSpec(memory_space=pltpu.SMEM)
    return pl.pallas_call(
        functools.partial(attend_kernel, width),
        grid=(2, peers // group),
        out_shape=jax.ShapeDtypeStruct((peers, rows, width + HD), BF16),
        in_specs=[
            smem,
            smem,
            pl.BlockSpec((group, CAP, width), lambda s, i: (i, s, 0)),
            pl.BlockSpec(memory_space=pltpu.VMEM),
        ],
        out_specs=pl.BlockSpec((group, CAP, width + HD), lambda s, i: (i, s, 0)),
        scratch_shapes=[
            pltpu.VMEM((peers * span, HD), BF16),
            pltpu.VMEM((peers * span, 2 * HD), BF16),
            pltpu.VMEM((m, peers * span), F32),
            pltpu.VMEM((m, 2 * HD), F32),
        ],
        compiler_params=pltpu.CompilerParams(vmem_limit_bytes=48 * 2**20),
        cost_estimate=pl.CostEstimate(
            flops=4 * peers * rows * G * 8 * span * HD,
            bytes_accessed=6 * 2**20,
            transcendentals=peers * rows * G * 8 * span,
        ),
        name=name,
    )(listed, count, q, kv)


def pages_here(owner):
    plane = owner.shape[0]
    mine = lax.axis_index("x") * 8 + lax.axis_index("y") + 4 * jnp.arange(2, dtype=jnp.int32)
    there = jnp.max((owner[None] == mine[:, None, None]).astype(jnp.int32), axis=2)
    peer = jnp.arange(plane, dtype=jnp.int32)
    rank = jnp.sum(there[:, None, :] * (peer[None, :] < peer[:, None]).astype(jnp.int32)[None], axis=2)
    hit = (there[:, None, :] == 1) & (rank[:, None, :] == peer[None, :, None])
    listed = jnp.sum(jnp.where(hit, peer[None, None, :], 0), axis=2)
    count = jnp.sum(there, axis=1)
    listed = jnp.where(peer[None, :] < count[:, None], listed, listed[:, :1])
    return listed.astype(jnp.int32), count.astype(jnp.int32)


def collect_kernel(col_ref, row_ref, replies_ref, out_ref):
    slot = slots_as_col(col_ref[...], row_ref[...])
    n, width = slot.shape[0], replies_ref.shape[1]
    pick = jnp.where(lax.broadcasted_iota(jnp.int32, (n, replies_ref.shape[0]), 1) == slot, 1.0, 0.0)
    rows = jnp.dot(pick.astype(BF16), replies_ref[...], preferred_element_type=F32).astype(BF16)
    out_ref[:, :width] = rows[: n // 2]
    out_ref[:, width:] = rows[n // 2 :]


def collect(ids_col, ids_row, replies):
    n = ids_col.shape[0]
    return pl.pallas_call(
        collect_kernel,
        out_shape=jax.ShapeDtypeStruct((n // 2, 2 * replies.shape[1]), BF16),
        compiler_params=pltpu.CompilerParams(vmem_limit_bytes=32 * 2**20),
        cost_estimate=pl.CostEstimate(
            flops=2 * n * replies.shape[0] * replies.shape[1], bytes_accessed=2**21, transcendentals=0
        ),
        name="collect",
    )(ids_col, ids_row, replies)


def merge_kernel(me_ref, col_ref, row_ref, own_ref, far_ref, suf_ref, suf_lse_ref, w_ref, send_ref, keep_ref, att_ref):
    @pl.when(pl.program_id(0) == 0)
    def _():
        n, width = suf_ref.shape
        slot = slots_as_col(col_ref[...], row_ref[...])
        pick = jnp.where(lax.broadcasted_iota(jnp.int32, (n, own_ref.shape[0]), 1) == slot, 1.0, 0.0)
        own = jnp.dot(pick.astype(BF16), own_ref[...], preferred_element_type=F32)
        far = jnp.concatenate([far_ref[:, : width + HD], far_ref[:, width + HD :]], axis=0)
        i = lax.broadcasted_iota(jnp.int32, (HD, width), 0)
        c = lax.broadcasted_iota(jnp.int32, (HD, width), 1)
        spread = jnp.where((i < 24) & ((i & 7) == (c >> 7)), 1.0, 0.0).astype(BF16)
        own_lse = jnp.dot(own[:, width:].astype(BF16), spread, preferred_element_type=F32)
        far_lse = jnp.dot(far[:, width:], spread, preferred_element_type=F32)
        suf_lse = suf_lse_ref[...]
        top = jnp.maximum(jnp.maximum(own_lse, far_lse), suf_lse)
        a = jnp.exp(own_lse - top)
        b = jnp.exp(far_lse - top)
        s = jnp.exp(suf_lse - top)
        att = (a * own[:, :width] + b * far[:, :width].astype(F32) + s * suf_ref[...]) / (a + b + s)
        att_ref[0] = att.astype(BF16)
        me = me_ref[0]
        step = n // 8
        for q in range(8):
            flip = (1 - q // 4) + 2 * (1 - (q // 2) % 2) + 4 * (1 - q % 2)
            at = pl.multiple_of((me ^ flip) * step, step)
            att_ref[1, q * step : (q + 1) * step] = att_ref[0, pl.ds(at, step), :]

    half = send_ref.shape[0]
    out = jnp.dot(att_ref[1], w_ref[...], preferred_element_type=F32).astype(BF16)
    send_ref[...] = out[:half]
    keep_ref[...] = out[half:]


def merge_project(me, ids_col, ids_row, own, far, suf, suf_lse, weight):
    n, width = suf.shape
    columns = weight.shape[1]
    tile = 512
    whole = pl.BlockSpec(memory_space=pltpu.VMEM)
    shape = jax.ShapeDtypeStruct((n // 2, columns), BF16)
    block = pl.BlockSpec((n // 2, tile), lambda c: (0, c))
    return pl.pallas_call(
        merge_kernel,
        grid=(columns // tile,),
        out_shape=(shape, shape),
        in_specs=[pl.BlockSpec(memory_space=pltpu.SMEM)]
        + [whole] * 6
        + [pl.BlockSpec((width, tile), lambda c: (0, c))],
        out_specs=(block, block),
        scratch_shapes=[pltpu.VMEM((2, n, width), BF16)],
        compiler_params=pltpu.CompilerParams(vmem_limit_bytes=40 * 2**20),
        cost_estimate=pl.CostEstimate(
            flops=2 * n * width * columns, bytes_accessed=16 * 2**20, transcendentals=3 * n * width
        ),
        name="merge_project",
    )(me, ids_col, ids_row, own, far, suf, suf_lse, weight)


def suffix_attend(queries, suffix_cache, suffix_len):
    seq, width = queries.shape
    rows = suffix_cache.shape[1]
    heads = queries.reshape(seq, width // HD, HD)
    scores = (
        jnp.einsum("sgd,std->sgt", heads, suffix_cache[:, :, 0], preferred_element_type=F32) * SCALE
    )
    in_length = (jnp.arange(rows, dtype=jnp.int32)[None, :] < suffix_len[:, None])[:, None, :]
    scores = jnp.where(in_length, scores, LOW)
    highest = jnp.max(scores, axis=-1)
    exp_terms = jnp.where(in_length, jnp.exp(scores - highest[..., None]), 0.0)
    totals = jnp.sum(exp_terms, axis=-1)
    out = (
        jnp.einsum("sgt,std->sgd", exp_terms.astype(BF16), suffix_cache[:, :, 1], preferred_element_type=F32)
        / totals[..., None]
    )
    lse = jnp.broadcast_to((highest + jnp.log(totals))[..., None], out.shape)
    return out.reshape(seq, width), lse.reshape(seq, width)


def swap(value, axis, bit):
    size = lax.axis_size(axis)
    return lax.ppermute(value, axis, [(i, i ^ bit) for i in range(size)])


def local(prefill_pages, page_owner, queries, suffix_cache, suffix_len, prefix_id, out_weight):
    plane = lax.axis_size("x") * lax.axis_size("y")
    pages, page = prefill_pages.shape[:2]
    seq, width = queries.shape
    pairs = pages // 2
    ids_col, ids_row = prefix_id, prefix_id.reshape(1, seq)
    far_row = swap(ids_row, "zh", 1)
    far_col = far_row.reshape(seq, 1)

    sent = dispatch(ids_col, ids_row, queries, plane * 2 * CAP).reshape(plane, 2 * CAP, width)
    own_q = lax.all_to_all(sent, PLANE, 0, 0, tiled=True)

    owner = page_owner[0, ::2]
    listed, count = pages_here(lax.all_gather(owner, PLANE))
    slot = slot_base(owner) // CAP
    here = jnp.arange(2 * plane, dtype=jnp.int32)[:, None] == slot[None, :]
    pick = jnp.sum(jnp.where(here, jnp.arange(pairs, dtype=jnp.int32)[None, :], 0), axis=1)
    paired = jnp.swapaxes(prefill_pages.reshape(pairs, 2 * page, 2, HD), 1, 2)
    paired = paired.reshape(pairs, 4 * page, HD)
    placed = place(pick, paired, 2 * plane).reshape(plane, 8 * page, HD)
    placed, own_q = lax.optimization_barrier((placed, own_q))
    kv = lax.all_to_all(placed, PLANE, 0, 0, tiled=True)
    far_q = swap(own_q, "zh", 1)

    suf, suf_lse = suffix_attend(queries, suffix_cache, suffix_len)
    far_q, suf, suf_lse, listed, count = lax.optimization_barrier((far_q, suf, suf_lse, listed, count))

    far_out = attend(listed, count, far_q, kv, "attend_far")
    far_out, own_q = lax.optimization_barrier((far_out, own_q))
    far_back = lax.all_to_all(far_out, PLANE, 0, 0, tiled=True)
    own_out = attend(listed, count, own_q, kv, "attend_own")
    far_back, own_out = lax.optimization_barrier((far_back, own_out))
    own_back = lax.all_to_all(own_out, PLANE, 0, 0, tiled=True)
    far_part = collect(far_col, far_row, far_back.reshape(plane * 2 * CAP, width + HD))
    far_part = swap(far_part, "zh", 1)

    me = (lax.axis_index("zl") * 2 + lax.axis_index("core")).astype(jnp.int32).reshape(1)
    send, keep = merge_project(
        me, ids_col, ids_row, own_back.reshape(plane * 2 * CAP, width + HD), far_part, suf, suf_lse, out_weight
    )

    def add(a, b):
        return (a.astype(F32) + b.astype(F32)).astype(BF16)

    got = swap(send, "core", 1)
    half = seq // 4
    send, keep = add(keep[:half], got[:half]), add(keep[half:], got[half:])
    got = swap(send, "zl", 1)
    half = seq // 8
    send, keep = add(keep[:half], got[:half]), add(keep[half:], got[half:])
    return add(keep, swap(send, "zl", 2))


def solution(mesh):
    x, zh, y, zl, core = 4, 2, 4, 4, 2
    names = ("x", "zh", "y", "zl", "core")
    fine = Mesh(mesh.devices.reshape(x, zh, y, zl, core), names)
    pool, tp = ("x", "zh", "y"), ("zl", "core")
    in_specs = (
        P(pool, None, None, tp),
        P(pool, None),
        P(pool, tp),
        P(pool, None, None, tp),
        P(pool),
        P(pool, None),
        P(tp, None),
    )
    out_specs = P(pool + tp, None)
    return jax.shard_map(local, mesh=fine, in_specs=in_specs, out_specs=out_specs, check_vma=False)
```

```python
import functools

import jax
import jax.numpy as jnp
from jax import lax
from jax.experimental import pallas as pl
from jax.experimental.pallas import tpu as pltpu
from jax.sharding import Mesh
from jax.sharding import PartitionSpec as P

HD = 128
G = 8
CAP = 16
PLANE = ("x", "y")
SCALE = HD**-0.5
LOG2E = 1.4426950408889634
LOW = -1e30
MARK = 16384.0
F32 = jnp.float32
BF16 = jnp.bfloat16


def slot_base(ids):
    return (((ids >> 3) * 4 + (ids & 3)) * 2 + ((ids >> 2) & 1)) * CAP


def slots_as_row(ids_col, ids_row):
    n = ids_row.shape[1]
    i = lax.broadcasted_iota(jnp.int32, (n, n), 0)
    j = lax.broadcasted_iota(jnp.int32, (n, n), 1)
    earlier = jnp.where((ids_col == ids_row) & (i < j), 1.0, 0.0)
    rank = jnp.sum(earlier, axis=0, keepdims=True).astype(jnp.int32)
    return slot_base(ids_row) + rank


def slots_as_col(ids_col, ids_row):
    n = ids_row.shape[1]
    i = lax.broadcasted_iota(jnp.int32, (n, n), 0)
    j = lax.broadcasted_iota(jnp.int32, (n, n), 1)
    earlier = jnp.where((ids_col == ids_row) & (j < i), 1.0, 0.0)
    rank = jnp.sum(earlier, axis=1, keepdims=True).astype(jnp.int32)
    return slot_base(ids_col) + rank


def dispatch_kernel(col_ref, row_ref, q_ref, out_ref):
    slot = slots_as_row(col_ref[...], row_ref[...])
    rows, n = out_ref.shape[0], slot.shape[1]
    pick = jnp.where(lax.broadcasted_iota(jnp.int32, (rows, n), 0) == slot, 1.0, 0.0)
    out_ref[...] = jnp.dot(pick.astype(BF16), q_ref[...], preferred_element_type=F32).astype(BF16)


def dispatch(ids_col, ids_row, queries, rows):
    return pl.pallas_call(
        dispatch_kernel,
        out_shape=jax.ShapeDtypeStruct((rows, queries.shape[1]), BF16),
        compiler_params=pltpu.CompilerParams(vmem_limit_bytes=32 * 2**20),
        cost_estimate=pl.CostEstimate(
            flops=2 * rows * queries.shape[0] * queries.shape[1], bytes_accessed=2**21, transcendentals=0
        ),
        name="dispatch",
    )(ids_col, ids_row, queries)


def place_kernel(pick_ref, pages_ref, out_ref):
    def one(slot, carry):
        src = pick_ref[slot]
        out_ref[slot] = pages_ref[jnp.maximum(src, 0)]

        @pl.when(src < 0)
        def _():
            out_ref[slot, :16, :] = jnp.full((16, HD), MARK, BF16)

        return carry

    lax.fori_loop(0, out_ref.shape[0], one, 0)


def place(pick, pages, slots):
    whole = pl.BlockSpec(memory_space=pltpu.VMEM)
    return pl.pallas_call(
        place_kernel,
        out_shape=jax.ShapeDtypeStruct((slots,) + pages.shape[1:], BF16),
        in_specs=[pl.BlockSpec(memory_space=pltpu.SMEM), whole],
        out_specs=whole,
        compiler_params=pltpu.CompilerParams(vmem_limit_bytes=32 * 2**20),
        cost_estimate=pl.CostEstimate(flops=0, bytes_accessed=6 * 2**20, transcendentals=0),
        name="place",
    )(pick, pages)


def attend_kernel(width, q_ref, kv_ref, out_ref, list_ref, key_ref, value_ref, s_ref, acc_ref):
    sub = pl.program_id(0)
    peers, span = kv_ref.shape[0], kv_ref.shape[1] // 4
    group, cap = q_ref.shape[0], q_ref.shape[1]
    key_at = pl.multiple_of(sub * 2 * span, 2 * span)

    @pl.when(pl.program_id(1) == 0)
    def _():
        there = [
            (jnp.max(kv_ref[src, pl.ds(key_at, 16), :].astype(F32)) < MARK / 2).astype(jnp.int32)
            for src in range(peers)
        ]
        count = jnp.int32(0)
        for src in range(peers):
            list_ref[count] = src
            count = count + there[src]
        list_ref[count] = list_ref[0]
        list_ref[peers + 1] = count
        even = ((count + 1) // 2) * 2

        def pack(n, carry):
            src = list_ref[n]
            at = pl.multiple_of(n * span, span)
            weight = jnp.where(n < count, 1.0, 0.0).astype(BF16)
            key_ref[pl.ds(at, span), :] = kv_ref[src, pl.ds(key_at, span), :]
            value_ref[pl.ds(at, span), :HD] = kv_ref[src, pl.ds(key_at + span, span), :] * weight
            value_ref[pl.ds(at, span), HD:] = jnp.full((span, HD), 1.0, BF16) * weight
            return carry

        lax.fori_loop(0, even, pack, 0)

    count = list_ref[peers + 1]
    even = ((count + 1) // 2) * 2
    heads = [(j, h) for j in range(group) for h in range(G)]
    q = jnp.concatenate([q_ref[j, :, h * HD : (h + 1) * HD] for j, h in heads], axis=0)
    fours = even // 4

    def score(at, size, top):
        key = key_ref[pl.ds(at, size), :]
        s = lax.dot_general(q, key, (((1,), (1,)), ((), ())), preferred_element_type=F32)
        s_ref[:, pl.ds(at, size)] = s
        for c in range(0, size, HD):
            top = jnp.maximum(top, s[:, c : c + HD])
        return top

    def four(i):
        return pl.multiple_of(i * 4 * span, 4 * span)

    def two(i):
        return pl.multiple_of(i * 2 * span, 2 * span)

    top = lax.fori_loop(
        0, fours, lambda i, t: score(four(i), 4 * span, t), jnp.full(q.shape, LOW, F32)
    )
    top = lax.fori_loop(2 * fours, even // 2, lambda i, t: score(two(i), 2 * span, t), top)
    top = jnp.max(top, axis=1, keepdims=True)
    acc_ref[...] = jnp.zeros_like(acc_ref)

    def weigh(at, size, carry):
        p = jnp.exp2((s_ref[:, pl.ds(at, size)] - top) * (SCALE * LOG2E)).astype(BF16)
        acc_ref[...] += jnp.dot(p, value_ref[pl.ds(at, size), :], preferred_element_type=F32)
        return carry

    lax.fori_loop(0, fours, lambda i, c: weigh(four(i), 4 * span, c), 0)
    lax.fori_loop(2 * fours, even // 2, lambda i, c: weigh(two(i), 2 * span, c), 0)
    total = acc_ref[:, HD:]
    total = jnp.where(total > 0.0, total, 1.0)
    out = (acc_ref[:, :HD] / total).astype(BF16)
    lane = lax.broadcasted_iota(jnp.int32, (cap, HD), 1)
    for j in range(group):
        packed_total = jnp.ones((cap, HD), F32)
        packed_top = jnp.zeros((cap, HD), F32)
        for h in range(G):
            at = (j * G + h) * cap
            out_ref[j, :, h * HD : (h + 1) * HD] = out[at : at + cap]
            packed_total = jnp.where((lane & 7) == h, total[at : at + cap], packed_total)
            packed_top = jnp.where((lane & 7) == h, top[at : at + cap], packed_top)
        lse = jnp.where(count > 0, packed_top * SCALE + jnp.log(packed_total), LOW)
        first = lse.astype(BF16).astype(F32)
        second = (lse - first).astype(BF16).astype(F32)
        third = lse - first - second
        part = jnp.where(lane < 8, first, jnp.where(lane < 16, second, third))
        out_ref[j, :, width:] = jnp.where(lane < 24, part, 0.0).astype(BF16)


def attend(q, kv, name):
    peers, rows, width = q.shape
    group = 8
    span = kv.shape[1] // 4
    m = group * CAP * G
    return pl.pallas_call(
        functools.partial(attend_kernel, width),
        grid=(2, peers // group),
        out_shape=jax.ShapeDtypeStruct((peers, rows, width + HD), BF16),
        in_specs=[
            pl.BlockSpec((group, CAP, width), lambda s, i: (i, s, 0)),
            pl.BlockSpec(memory_space=pltpu.VMEM),
        ],
        out_specs=pl.BlockSpec((group, CAP, width + HD), lambda s, i: (i, s, 0)),
        scratch_shapes=[
            pltpu.SMEM((peers + 2,), jnp.int32),
            pltpu.VMEM((peers * span, HD), BF16),
            pltpu.VMEM((peers * span, 2 * HD), BF16),
            pltpu.VMEM((m, peers * span), F32),
            pltpu.VMEM((m, 2 * HD), F32),
        ],
        compiler_params=pltpu.CompilerParams(vmem_limit_bytes=48 * 2**20),
        cost_estimate=pl.CostEstimate(
            flops=4 * peers * rows * G * 8 * span * HD,
            bytes_accessed=6 * 2**20,
            transcendentals=peers * rows * G * 8 * span,
        ),
        name=name,
    )(q, kv)


def collect_kernel(col_ref, row_ref, replies_ref, out_ref):
    slot = slots_as_col(col_ref[...], row_ref[...])
    n, width = slot.shape[0], replies_ref.shape[1]
    pick = jnp.where(lax.broadcasted_iota(jnp.int32, (n, replies_ref.shape[0]), 1) == slot, 1.0, 0.0)
    rows = jnp.dot(pick.astype(BF16), replies_ref[...], preferred_element_type=F32).astype(BF16)
    out_ref[:, :width] = rows[: n // 2]
    out_ref[:, width:] = rows[n // 2 :]


def collect(ids_col, ids_row, replies):
    n = ids_col.shape[0]
    return pl.pallas_call(
        collect_kernel,
        out_shape=jax.ShapeDtypeStruct((n // 2, 2 * replies.shape[1]), BF16),
        compiler_params=pltpu.CompilerParams(vmem_limit_bytes=32 * 2**20),
        cost_estimate=pl.CostEstimate(
            flops=2 * n * replies.shape[0] * replies.shape[1], bytes_accessed=2**21, transcendentals=0
        ),
        name="collect",
    )(ids_col, ids_row, replies)


def merge_kernel(me_ref, col_ref, row_ref, own_ref, far_ref, suf_ref, suf_lse_ref, w_ref, send_ref, keep_ref, att_ref, w_buf, sem):
    tile = w_ref.shape[1] // sem.shape[0]
    fetches = [
        pltpu.make_async_copy(
            w_ref.at[:, pl.ds(t * tile, tile)], w_buf.at[:, pl.ds(t * tile, tile)], sem.at[t]
        )
        for t in range(sem.shape[0])
    ]
    for fetch in fetches:
        fetch.start()
    n, width = suf_ref.shape
    slot = slots_as_col(col_ref[...], row_ref[...])
    pick = jnp.where(lax.broadcasted_iota(jnp.int32, (n, own_ref.shape[0]), 1) == slot, 1.0, 0.0)
    own = jnp.dot(pick.astype(BF16), own_ref[...], preferred_element_type=F32)
    far = jnp.concatenate([far_ref[:, : width + HD], far_ref[:, width + HD :]], axis=0)
    i = lax.broadcasted_iota(jnp.int32, (HD, width), 0)
    c = lax.broadcasted_iota(jnp.int32, (HD, width), 1)
    spread = jnp.where((i < 24) & ((i & 7) == (c >> 7)), 1.0, 0.0).astype(BF16)
    own_lse = jnp.dot(own[:, width:].astype(BF16), spread, preferred_element_type=F32)
    far_lse = jnp.dot(far[:, width:], spread, preferred_element_type=F32)
    suf_lse = suf_lse_ref[...]
    top = jnp.maximum(jnp.maximum(own_lse, far_lse), suf_lse)
    a = jnp.exp(own_lse - top)
    b = jnp.exp(far_lse - top)
    s = jnp.exp(suf_lse - top)
    att = (a * own[:, :width] + b * far[:, :width].astype(F32) + s * suf_ref[...]) / (a + b + s)
    att_ref[0] = att.astype(BF16)
    me = me_ref[0]
    step = n // 8
    for q in range(8):
        flip = (1 - q // 4) + 2 * (1 - (q // 2) % 2) + 4 * (1 - q % 2)
        at = pl.multiple_of((me ^ flip) * step, step)
        att_ref[1, q * step : (q + 1) * step] = att_ref[0, pl.ds(at, step), :]
    half = send_ref.shape[0]
    for t, fetch in enumerate(fetches):
        fetch.wait()
        out = jnp.dot(
            att_ref[1], w_buf[:, t * tile : (t + 1) * tile], preferred_element_type=F32
        ).astype(BF16)
        send_ref[:, t * tile : (t + 1) * tile] = out[:half]
        keep_ref[:, t * tile : (t + 1) * tile] = out[half:]


def merge_project(me, ids_col, ids_row, own, far, suf, suf_lse, weight):
    n, width = suf.shape
    columns = weight.shape[1]
    whole = pl.BlockSpec(memory_space=pltpu.VMEM)
    shape = jax.ShapeDtypeStruct((n // 2, columns), BF16)
    return pl.pallas_call(
        merge_kernel,
        out_shape=(shape, shape),
        in_specs=[pl.BlockSpec(memory_space=pltpu.SMEM)]
        + [whole] * 6
        + [pl.BlockSpec(memory_space=pl.ANY)],
        out_specs=(whole, whole),
        scratch_shapes=[
            pltpu.VMEM((2, n, width), BF16),
            pltpu.VMEM(weight.shape, BF16),
            pltpu.SemaphoreType.DMA((8,)),
        ],
        compiler_params=pltpu.CompilerParams(vmem_limit_bytes=48 * 2**20),
        cost_estimate=pl.CostEstimate(
            flops=2 * n * width * columns, bytes_accessed=16 * 2**20, transcendentals=3 * n * width
        ),
        name="merge_project",
    )(me, ids_col, ids_row, own, far, suf, suf_lse, weight)


def suffix_attend(queries, suffix_cache, suffix_len):
    seq, width = queries.shape
    rows = suffix_cache.shape[1]
    heads = queries.reshape(seq, width // HD, HD)
    scores = (
        jnp.einsum("sgd,std->sgt", heads, suffix_cache[:, :, 0], preferred_element_type=F32) * SCALE
    )
    in_length = (jnp.arange(rows, dtype=jnp.int32)[None, :] < suffix_len[:, None])[:, None, :]
    scores = jnp.where(in_length, scores, LOW)
    highest = jnp.max(scores, axis=-1)
    exp_terms = jnp.where(in_length, jnp.exp(scores - highest[..., None]), 0.0)
    totals = jnp.sum(exp_terms, axis=-1)
    out = (
        jnp.einsum("sgt,std->sgd", exp_terms.astype(BF16), suffix_cache[:, :, 1], preferred_element_type=F32)
        / totals[..., None]
    )
    lse = jnp.broadcast_to((highest + jnp.log(totals))[..., None], out.shape)
    return out.reshape(seq, width), lse.reshape(seq, width)


def swap(value, axis, bit):
    size = lax.axis_size(axis)
    return lax.ppermute(value, axis, [(i, i ^ bit) for i in range(size)])


def local(prefill_pages, page_owner, queries, suffix_cache, suffix_len, prefix_id, out_weight):
    plane = lax.axis_size("x") * lax.axis_size("y")
    pages, page = prefill_pages.shape[:2]
    seq, width = queries.shape
    pairs = pages // 2
    ids_col, ids_row = prefix_id, prefix_id.reshape(1, seq)
    far_row = swap(ids_row, "zh", 1)

    sent = dispatch(ids_col, ids_row, queries, plane * 2 * CAP).reshape(plane, 2 * CAP, width)
    own_q = lax.all_to_all(sent, PLANE, 0, 0, tiled=True)

    owner = page_owner[0, ::2]
    slot = slot_base(owner) // CAP
    here = jnp.arange(2 * plane, dtype=jnp.int32)[:, None] == slot[None, :]
    pick = jnp.sum(jnp.where(here, jnp.arange(pairs, dtype=jnp.int32)[None, :] + 1, 0), axis=1) - 1
    paired = jnp.swapaxes(prefill_pages.reshape(pairs, 2 * page, 2, HD), 1, 2)
    paired = paired.reshape(pairs, 4 * page, HD)
    placed = place(pick, paired, 2 * plane).reshape(plane, 8 * page, HD)
    placed, own_q, far_row, later = lax.optimization_barrier((placed, own_q, far_row, queries))
    far_col = far_row.reshape(seq, 1)
    kv = lax.all_to_all(placed, PLANE, 0, 0, tiled=True)
    far_q = swap(own_q, "zh", 1)

    suf, suf_lse = suffix_attend(later, suffix_cache, suffix_len)
    far_q, suf, suf_lse = lax.optimization_barrier((far_q, suf, suf_lse))

    far_out = attend(far_q, kv, "attend_far")
    far_out, own_q = lax.optimization_barrier((far_out, own_q))
    far_back = lax.all_to_all(far_out, PLANE, 0, 0, tiled=True)
    own_out = attend(own_q, kv, "attend_own")
    far_back, own_out = lax.optimization_barrier((far_back, own_out))
    own_back = lax.all_to_all(own_out, PLANE, 0, 0, tiled=True)
    far_part = collect(far_col, far_row, far_back.reshape(plane * 2 * CAP, width + HD))
    far_part = swap(far_part, "zh", 1)

    me = (lax.axis_index("zl") * 2 + lax.axis_index("core")).astype(jnp.int32).reshape(1)
    send, keep = merge_project(
        me, ids_col, ids_row, own_back.reshape(plane * 2 * CAP, width + HD), far_part, suf, suf_lse, out_weight
    )

    def add(a, b):
        return (a.astype(F32) + b.astype(F32)).astype(BF16)

    got = swap(send, "core", 1)
    half = seq // 4
    send, keep = add(keep[:half], got[:half]), add(keep[half:], got[half:])
    got = swap(send, "zl", 1)
    half = seq // 8
    send, keep = add(keep[:half], got[:half]), add(keep[half:], got[half:])
    return add(keep, swap(send, "zl", 2))


def solution(mesh):
    x, zh, y, zl, core = 4, 2, 4, 4, 2
    names = ("x", "zh", "y", "zl", "core")
    fine = Mesh(mesh.devices.reshape(x, zh, y, zl, core), names)
    pool, tp = ("x", "zh", "y"), ("zl", "core")
    in_specs = (
        P(pool, None, None, tp),
        P(pool, None),
        P(pool, tp),
        P(pool, None, None, tp),
        P(pool),
        P(pool, None),
        P(tp, None),
    )
    out_specs = P(pool + tp, None)
    return jax.shard_map(local, mesh=fine, in_specs=in_specs, out_specs=out_specs, check_vma=False)
```

```python
import functools

import jax
import jax.numpy as jnp
from jax import lax
from jax.experimental import pallas as pl
from jax.experimental.pallas import tpu as pltpu
from jax.sharding import Mesh
from jax.sharding import PartitionSpec as P

HD = 128
G = 8
CAP = 16
PLANE = ("x", "y")
SCALE = HD**-0.5
LOG2E = 1.4426950408889634
LOW = -1e30
MARK = 16384.0
F32 = jnp.float32
BF16 = jnp.bfloat16


def slot_base(ids):
    return (((ids >> 3) * 4 + (ids & 3)) * 2 + ((ids >> 2) & 1)) * CAP


def slots_as_row(ids_col, ids_row):
    n = ids_row.shape[1]
    i = lax.broadcasted_iota(jnp.int32, (n, n), 0)
    j = lax.broadcasted_iota(jnp.int32, (n, n), 1)
    earlier = jnp.where((ids_col == ids_row) & (i < j), 1.0, 0.0)
    rank = jnp.sum(earlier, axis=0, keepdims=True).astype(jnp.int32)
    return slot_base(ids_row) + rank


def slots_as_col(ids_col, ids_row):
    n = ids_row.shape[1]
    i = lax.broadcasted_iota(jnp.int32, (n, n), 0)
    j = lax.broadcasted_iota(jnp.int32, (n, n), 1)
    earlier = jnp.where((ids_col == ids_row) & (j < i), 1.0, 0.0)
    rank = jnp.sum(earlier, axis=1, keepdims=True).astype(jnp.int32)
    return slot_base(ids_col) + rank


def dispatch_kernel(col_ref, row_ref, q_ref, out_ref):
    slot = slots_as_row(col_ref[...], row_ref[...])
    rows, n = out_ref.shape[0], slot.shape[1]
    pick = jnp.where(lax.broadcasted_iota(jnp.int32, (rows, n), 0) == slot, 1.0, 0.0)
    out_ref[...] = jnp.dot(pick.astype(BF16), q_ref[...], preferred_element_type=F32).astype(BF16)


def dispatch(ids_col, ids_row, queries, rows):
    return pl.pallas_call(
        dispatch_kernel,
        out_shape=jax.ShapeDtypeStruct((rows, queries.shape[1]), BF16),
        compiler_params=pltpu.CompilerParams(vmem_limit_bytes=32 * 2**20),
        cost_estimate=pl.CostEstimate(
            flops=2 * rows * queries.shape[0] * queries.shape[1], bytes_accessed=2**21, transcendentals=0
        ),
        name="dispatch",
    )(ids_col, ids_row, queries)


def place_kernel(pick_ref, pages_ref, out_ref):
    def one(slot, carry):
        src = pick_ref[slot]
        out_ref[slot] = pages_ref[jnp.maximum(src, 0)]

        @pl.when(src < 0)
        def _():
            out_ref[slot, :16, :] = jnp.full((16, HD), MARK, BF16)

        return carry

    lax.fori_loop(0, out_ref.shape[0], one, 0)


def place(pick, pages, slots):
    whole = pl.BlockSpec(memory_space=pltpu.VMEM)
    return pl.pallas_call(
        place_kernel,
        out_shape=jax.ShapeDtypeStruct((slots,) + pages.shape[1:], BF16),
        in_specs=[pl.BlockSpec(memory_space=pltpu.SMEM), whole],
        out_specs=whole,
        compiler_params=pltpu.CompilerParams(vmem_limit_bytes=32 * 2**20),
        cost_estimate=pl.CostEstimate(flops=0, bytes_accessed=6 * 2**20, transcendentals=0),
        name="place",
    )(pick, pages)


def attend_kernel(width, first, q_ref, kv_ref, *refs):
    out_ref, list_ref, key_ref, value_ref, s_ref, acc_ref = refs[-6:]
    sub = pl.program_id(0) + first
    peers, span = kv_ref.shape[0], kv_ref.shape[1] // 4
    group, cap = q_ref.shape[0], q_ref.shape[1]
    key_at = pl.multiple_of(sub * 2 * span, 2 * span)

    @pl.when(pl.program_id(1) == 0)
    def _():
        there = [
            (jnp.max(kv_ref[src, pl.ds(key_at, 16), :].astype(F32)) < MARK / 2).astype(jnp.int32)
            for src in range(peers)
        ]
        count = jnp.int32(0)
        for src in range(peers):
            list_ref[count] = src
            count = count + there[src]
        list_ref[count] = list_ref[0]
        list_ref[peers + 1] = count
        even = ((count + 1) // 2) * 2

        def pack(n, carry):
            src = list_ref[n]
            at = pl.multiple_of(n * span, span)
            weight = jnp.where(n < count, 1.0, 0.0).astype(BF16)
            key_ref[pl.ds(at, span), :] = kv_ref[src, pl.ds(key_at, span), :]
            value_ref[pl.ds(at, span), :HD] = kv_ref[src, pl.ds(key_at + span, span), :] * weight
            value_ref[pl.ds(at, span), HD:] = jnp.full((span, HD), 1.0, BF16) * weight
            return carry

        lax.fori_loop(0, even, pack, 0)

    count = list_ref[peers + 1]
    even = ((count + 1) // 2) * 2
    heads = [(j, h) for j in range(group) for h in range(G)]
    q = jnp.concatenate([q_ref[j, :, h * HD : (h + 1) * HD] for j, h in heads], axis=0)
    fours = even // 4

    def score(at, size, top):
        key = key_ref[pl.ds(at, size), :]
        s = lax.dot_general(q, key, (((1,), (1,)), ((), ())), preferred_element_type=F32)
        s_ref[:, pl.ds(at, size)] = s
        for c in range(0, size, HD):
            top = jnp.maximum(top, s[:, c : c + HD])
        return top

    def four(i):
        return pl.multiple_of(i * 4 * span, 4 * span)

    def two(i):
        return pl.multiple_of(i * 2 * span, 2 * span)

    top = lax.fori_loop(
        0, fours, lambda i, t: score(four(i), 4 * span, t), jnp.full(q.shape, LOW, F32)
    )
    top = lax.fori_loop(2 * fours, even // 2, lambda i, t: score(two(i), 2 * span, t), top)
    top = jnp.max(top, axis=1, keepdims=True)
    acc_ref[...] = jnp.zeros_like(acc_ref)

    def weigh(at, size, carry):
        p = jnp.exp2((s_ref[:, pl.ds(at, size)] - top) * (SCALE * LOG2E)).astype(BF16)
        acc_ref[...] += jnp.dot(p, value_ref[pl.ds(at, size), :], preferred_element_type=F32)
        return carry

    lax.fori_loop(0, fours, lambda i, c: weigh(four(i), 4 * span, c), 0)
    lax.fori_loop(2 * fours, even // 2, lambda i, c: weigh(two(i), 2 * span, c), 0)
    total = acc_ref[:, HD:]
    total = jnp.where(total > 0.0, total, 1.0)
    out = (acc_ref[:, :HD] / total).astype(BF16)
    lane = lax.broadcasted_iota(jnp.int32, (cap, HD), 1)
    for j in range(group):
        packed_total = jnp.ones((cap, HD), F32)
        packed_top = jnp.zeros((cap, HD), F32)
        for h in range(G):
            at = (j * G + h) * cap
            out_ref[j, :, h * HD : (h + 1) * HD] = out[at : at + cap]
            packed_total = jnp.where((lane & 7) == h, total[at : at + cap], packed_total)
            packed_top = jnp.where((lane & 7) == h, top[at : at + cap], packed_top)
        lse = jnp.where(count > 0, packed_top * SCALE + jnp.log(packed_total), LOW)
        first = lse.astype(BF16).astype(F32)
        second = (lse - first).astype(BF16).astype(F32)
        third = lse - first - second
        part = jnp.where(lane < 8, first, jnp.where(lane < 16, second, third))
        out_ref[j, :, width:] = jnp.where(lane < 24, part, 0.0).astype(BF16)


def attend(q, kv, name, first, number, begun=None):
    peers, rows, width = q.shape
    group = 8
    span = kv.shape[1] // 4
    m = group * CAP * G
    return pl.pallas_call(
        functools.partial(attend_kernel, width, first),
        grid=(number, peers // group),
        out_shape=jax.ShapeDtypeStruct((peers, rows, width + HD), BF16),
        in_specs=[
            pl.BlockSpec((group, CAP, width), lambda s, i: (i, s + first, 0)),
            pl.BlockSpec(memory_space=pltpu.VMEM),
        ]
        + [pl.BlockSpec(memory_space=pl.ANY)] * (begun is not None),
        out_specs=pl.BlockSpec((group, CAP, width + HD), lambda s, i: (i, s + first, 0)),
        input_output_aliases={} if begun is None else {2: 0},
        scratch_shapes=[
            pltpu.SMEM((peers + 2,), jnp.int32),
            pltpu.VMEM((peers * span, HD), BF16),
            pltpu.VMEM((peers * span, 2 * HD), BF16),
            pltpu.VMEM((m, peers * span), F32),
            pltpu.VMEM((m, 2 * HD), F32),
        ],
        compiler_params=pltpu.CompilerParams(vmem_limit_bytes=34 * 2**20),
        cost_estimate=pl.CostEstimate(
            flops=2 * number * peers * rows * G * 8 * span * HD,
            bytes_accessed=3 * number * 2**20,
            transcendentals=number * peers * rows * G * 4 * span,
        ),
        name=name,
    )(*((q, kv) if begun is None else (q, kv, begun)))


def collect_kernel(col_ref, row_ref, replies_ref, low_ref, high_ref):
    slot = slots_as_col(col_ref[...], row_ref[...])
    n, width = slot.shape[0], replies_ref.shape[1]
    pick = jnp.where(lax.broadcasted_iota(jnp.int32, (n, replies_ref.shape[0]), 1) == slot, 1.0, 0.0)
    rows = jnp.dot(pick.astype(BF16), replies_ref[...], preferred_element_type=F32).astype(BF16)
    for ref, at in ((low_ref, 0), (high_ref, n // 2)):
        ref[:, :width] = rows[at : at + n // 4]
        ref[:, width:] = rows[at + n // 4 : at + n // 2]


def collect(ids_col, ids_row, replies):
    n = ids_col.shape[0]
    return pl.pallas_call(
        collect_kernel,
        out_shape=(jax.ShapeDtypeStruct((n // 4, 2 * replies.shape[1]), BF16),) * 2,
        compiler_params=pltpu.CompilerParams(vmem_limit_bytes=32 * 2**20),
        cost_estimate=pl.CostEstimate(
            flops=2 * n * replies.shape[0] * replies.shape[1], bytes_accessed=2**21, transcendentals=0
        ),
        name="collect",
    )(ids_col, ids_row, replies)


def fetch_weight(w_ref, w_buf, sem, first):
    tile = w_buf.shape[1] // sem.shape[0]
    fetches = [
        pltpu.make_async_copy(
            w_ref.at[:, pl.ds(first + t * tile, tile)], w_buf.at[:, pl.ds(t * tile, tile)], sem.at[t]
        )
        for t in range(sem.shape[0])
    ]
    for fetch in fetches:
        fetch.start()
    return fetches


def project(fetches, att_ref, w_buf, send_ref, keep_ref):
    half = send_ref.shape[0]
    tile = w_buf.shape[1] // len(fetches)
    for t, fetch in enumerate(fetches):
        fetch.wait()
        out = jnp.dot(
            att_ref[...], w_buf[:, t * tile : (t + 1) * tile], preferred_element_type=F32
        ).astype(BF16)
        send_ref[:, t * tile : (t + 1) * tile] = out[:half]
        keep_ref[:, t * tile : (t + 1) * tile] = out[half:]


def merge_kernel(me_ref, col_ref, row_ref, own_ref, low_ref, high_ref, suf_ref, suf_lse_ref, w_ref, att_ref, send_ref, keep_ref, plain_ref, w_buf, sem):
    fetches = fetch_weight(w_ref, w_buf, sem, 0)
    n, width = suf_ref.shape
    slot = slots_as_col(col_ref[...], row_ref[...])
    pick = jnp.where(lax.broadcasted_iota(jnp.int32, (n, own_ref.shape[0]), 1) == slot, 1.0, 0.0)
    own = jnp.dot(pick.astype(BF16), own_ref[...], preferred_element_type=F32)
    cut = width + HD
    far = jnp.concatenate([low_ref[:, :cut], low_ref[:, cut:], high_ref[:, :cut], high_ref[:, cut:]], axis=0)
    i = lax.broadcasted_iota(jnp.int32, (HD, width), 0)
    c = lax.broadcasted_iota(jnp.int32, (HD, width), 1)
    spread = jnp.where((i < 24) & ((i & 7) == (c >> 7)), 1.0, 0.0).astype(BF16)
    own_lse = jnp.dot(own[:, width:].astype(BF16), spread, preferred_element_type=F32)
    far_lse = jnp.dot(far[:, width:], spread, preferred_element_type=F32)
    suf_lse = suf_lse_ref[...]
    top = jnp.maximum(jnp.maximum(own_lse, far_lse), suf_lse)
    a = jnp.exp(own_lse - top)
    b = jnp.exp(far_lse - top)
    s = jnp.exp(suf_lse - top)
    att = (a * own[:, :width] + b * far[:, :width].astype(F32) + s * suf_ref[...]) / (a + b + s)
    plain_ref[...] = att.astype(BF16)
    me = me_ref[0]
    step = n // 8
    for q in range(8):
        flip = (1 - q // 4) + 2 * (1 - (q // 2) % 2) + 4 * (1 - q % 2)
        at = pl.multiple_of((me ^ flip) * step, step)
        att_ref[q * step : (q + 1) * step] = plain_ref[pl.ds(at, step), :]
    project(fetches, att_ref, w_buf, send_ref, keep_ref)


def project_kernel(first, att_ref, w_ref, send_ref, keep_ref, w_buf, sem):
    project(fetch_weight(w_ref, w_buf, sem, first), att_ref, w_buf, send_ref, keep_ref)


def merge_project(me, ids_col, ids_row, own, low, high, suf, suf_lse, weight):
    n, width = suf.shape
    columns = weight.shape[1] // 2
    whole = pl.BlockSpec(memory_space=pltpu.VMEM)
    shape = jax.ShapeDtypeStruct((n // 2, columns), BF16)
    scratch = [pltpu.VMEM((width, columns), BF16), pltpu.SemaphoreType.DMA((4,))]
    params = pltpu.CompilerParams(vmem_limit_bytes=56 * 2**20)
    cost = pl.CostEstimate(flops=2 * n * width * columns, bytes_accessed=8 * 2**20, transcendentals=n * width)
    att, send_a, keep_a = pl.pallas_call(
        merge_kernel,
        out_shape=(jax.ShapeDtypeStruct((n, width), BF16), shape, shape),
        in_specs=[pl.BlockSpec(memory_space=pltpu.SMEM)]
        + [whole] * 7
        + [pl.BlockSpec(memory_space=pl.ANY)],
        out_specs=(whole, whole, whole),
        scratch_shapes=[pltpu.VMEM((n, width), BF16)] + scratch,
        compiler_params=params,
        cost_estimate=cost,
        name="merge_project",
    )(me, ids_col, ids_row, own, low, high, suf, suf_lse, weight)
    send_b, keep_b = pl.pallas_call(
        functools.partial(project_kernel, columns),
        out_shape=(shape, shape),
        in_specs=[whole, pl.BlockSpec(memory_space=pl.ANY)],
        out_specs=(whole, whole),
        scratch_shapes=scratch,
        compiler_params=params,
        cost_estimate=cost,
        name="project",
    )(att, weight)
    return (send_a, keep_a), (send_b, keep_b)


def suffix_attend(queries, suffix_cache, suffix_len):
    seq, width = queries.shape
    rows = suffix_cache.shape[1]
    heads = queries.reshape(seq, width // HD, HD)
    scores = (
        jnp.einsum("sgd,std->sgt", heads, suffix_cache[:, :, 0], preferred_element_type=F32) * SCALE
    )
    in_length = (jnp.arange(rows, dtype=jnp.int32)[None, :] < suffix_len[:, None])[:, None, :]
    scores = jnp.where(in_length, scores, LOW)
    highest = jnp.max(scores, axis=-1)
    exp_terms = jnp.where(in_length, jnp.exp(scores - highest[..., None]), 0.0)
    totals = jnp.sum(exp_terms, axis=-1)
    out = (
        jnp.einsum("sgt,std->sgd", exp_terms.astype(BF16), suffix_cache[:, :, 1], preferred_element_type=F32)
        / totals[..., None]
    )
    lse = jnp.broadcast_to((highest + jnp.log(totals))[..., None], out.shape)
    return out.reshape(seq, width), lse.reshape(seq, width)


def swap(value, axis, bit):
    size = lax.axis_size(axis)
    return lax.ppermute(value, axis, [(i, i ^ bit) for i in range(size)])


def local(prefill_pages, page_owner, queries, suffix_cache, suffix_len, prefix_id, out_weight):
    plane = lax.axis_size("x") * lax.axis_size("y")
    pages, page = prefill_pages.shape[:2]
    seq, width = queries.shape
    pairs = pages // 2
    ids_col, ids_row = prefix_id, prefix_id.reshape(1, seq)
    far_row = swap(ids_row, "zh", 1)

    sent = dispatch(ids_col, ids_row, queries, plane * 2 * CAP).reshape(plane, 2 * CAP, width)
    own_q = lax.all_to_all(sent, PLANE, 0, 0, tiled=True)

    owner = page_owner[0, ::2]
    slot = slot_base(owner) // CAP
    here = jnp.arange(2 * plane, dtype=jnp.int32)[:, None] == slot[None, :]
    pick = jnp.sum(jnp.where(here, jnp.arange(pairs, dtype=jnp.int32)[None, :] + 1, 0), axis=1) - 1
    paired = jnp.swapaxes(prefill_pages.reshape(pairs, 2 * page, 2, HD), 1, 2)
    paired = paired.reshape(pairs, 4 * page, HD)
    placed = place(pick, paired, 2 * plane).reshape(plane, 8 * page, HD)
    placed, own_q, far_row, later = lax.optimization_barrier((placed, own_q, far_row, queries))
    far_col = far_row.reshape(seq, 1)
    kv = lax.all_to_all(placed, PLANE, 0, 0, tiled=True)
    far_q = swap(own_q, "zh", 1)

    suf, suf_lse = suffix_attend(later, suffix_cache, suffix_len)
    far_q, suf, suf_lse = lax.optimization_barrier((far_q, suf, suf_lse))

    far_out = attend(far_q, kv, "attend_far", 0, 2)
    far_out, own_q = lax.optimization_barrier((far_out, own_q))
    far_back = lax.all_to_all(far_out, PLANE, 0, 0, tiled=True)
    own_out = attend(own_q, kv, "attend_own", 0, 1)
    far_back, own_out = lax.optimization_barrier((far_back, own_out))
    far_part = collect(far_col, far_row, far_back.reshape(plane * 2 * CAP, width + HD))
    far_part, own_out = lax.optimization_barrier((far_part, own_out))
    far_low = swap(far_part[0], "zh", 1)
    far_high = swap(far_part[1], "zh", 1)
    own_out = attend(own_q, kv, "attend_own", 1, 1, own_out)
    far_low, own_out = lax.optimization_barrier((far_low, own_out))
    own_back = lax.all_to_all(own_out, PLANE, 0, 0, tiled=True)

    me = (lax.axis_index("zl") * 2 + lax.axis_index("core")).astype(jnp.int32).reshape(1)
    halves = merge_project(
        me, ids_col, ids_row, own_back.reshape(plane * 2 * CAP, width + HD), far_low, far_high, suf, suf_lse, out_weight
    )

    def add(a, b):
        return (a.astype(F32) + b.astype(F32)).astype(BF16)

    def fold(send, keep, axis, bit):
        got = swap(send, axis, bit)
        half = keep.shape[0] // 2
        return add(keep[:half], got[:half]), add(keep[half:], got[half:])

    halves = [fold(send, keep, "core", 1) for send, keep in halves]
    halves = [fold(send, keep, "zl", 1) for send, keep in halves]
    return jnp.concatenate([add(keep, swap(send, "zl", 2)) for send, keep in halves], axis=1)


def solution(mesh):
    x, zh, y, zl, core = 4, 2, 4, 4, 2
    names = ("x", "zh", "y", "zl", "core")
    fine = Mesh(mesh.devices.reshape(x, zh, y, zl, core), names)
    pool, tp = ("x", "zh", "y"), ("zl", "core")
    in_specs = (
        P(pool, None, None, tp),
        P(pool, None),
        P(pool, tp),
        P(pool, None, None, tp),
        P(pool),
        P(pool, None),
        P(tp, None),
    )
    out_specs = P(pool + tp, None)
    return jax.shard_map(local, mesh=fine, in_specs=in_specs, out_specs=out_specs, check_vma=False)
```

```python
import functools

import jax
import jax.numpy as jnp
from jax import lax
from jax.experimental import pallas as pl
from jax.experimental.pallas import tpu as pltpu
from jax.sharding import Mesh
from jax.sharding import PartitionSpec as P

HD = 128
G = 8
CAP = 16
PLANE = ("x", "y")
SCALE = HD**-0.5
LOG2E = 1.4426950408889634
LOW = -1e30
MARK = 16384.0
F32 = jnp.float32
BF16 = jnp.bfloat16


def slot_base(ids):
    return (((ids >> 3) * 4 + (ids & 3)) * 2 + ((ids >> 2) & 1)) * CAP


def slots_as_row(ids_col, ids_row):
    n = ids_row.shape[1]
    i = lax.broadcasted_iota(jnp.int32, (n, n), 0)
    j = lax.broadcasted_iota(jnp.int32, (n, n), 1)
    earlier = jnp.where((ids_col == ids_row) & (i < j), 1.0, 0.0)
    rank = jnp.sum(earlier, axis=0, keepdims=True).astype(jnp.int32)
    return slot_base(ids_row) + rank


def slots_as_col(ids_col, ids_row):
    n = ids_row.shape[1]
    i = lax.broadcasted_iota(jnp.int32, (n, n), 0)
    j = lax.broadcasted_iota(jnp.int32, (n, n), 1)
    earlier = jnp.where((ids_col == ids_row) & (j < i), 1.0, 0.0)
    rank = jnp.sum(earlier, axis=1, keepdims=True).astype(jnp.int32)
    return slot_base(ids_col) + rank


def dispatch_kernel(col_ref, row_ref, q_ref, out_ref):
    slot = slots_as_row(col_ref[...], row_ref[...])
    rows, n = out_ref.shape[0], slot.shape[1]
    pick = jnp.where(lax.broadcasted_iota(jnp.int32, (rows, n), 0) == slot, 1.0, 0.0)
    out_ref[...] = jnp.dot(pick.astype(BF16), q_ref[...], preferred_element_type=F32).astype(BF16)


def dispatch(ids_col, ids_row, queries, rows):
    return pl.pallas_call(
        dispatch_kernel,
        out_shape=jax.ShapeDtypeStruct((rows, queries.shape[1]), BF16),
        compiler_params=pltpu.CompilerParams(vmem_limit_bytes=32 * 2**20),
        cost_estimate=pl.CostEstimate(
            flops=2 * rows * queries.shape[0] * queries.shape[1], bytes_accessed=2**21, transcendentals=0
        ),
        name="dispatch",
    )(ids_col, ids_row, queries)


def place_kernel(pick_ref, pages_ref, *out_refs):
    for sub, out_ref in enumerate(out_refs):

        def one(group, carry):
            src = pick_ref[2 * group + sub]
            out_ref[group] = pages_ref[jnp.maximum(src, 0)]

            @pl.when(src < 0)
            def _():
                out_ref[group, :16, :] = jnp.full((16, HD), MARK, BF16)

            return carry

        lax.fori_loop(0, out_ref.shape[0], one, 0)


def place(pick, pages, plane):
    whole = pl.BlockSpec(memory_space=pltpu.VMEM)
    return pl.pallas_call(
        place_kernel,
        out_shape=(jax.ShapeDtypeStruct((plane,) + pages.shape[1:], BF16),) * 2,
        in_specs=[pl.BlockSpec(memory_space=pltpu.SMEM), whole],
        out_specs=(whole, whole),
        compiler_params=pltpu.CompilerParams(vmem_limit_bytes=32 * 2**20),
        cost_estimate=pl.CostEstimate(flops=0, bytes_accessed=6 * 2**20, transcendentals=0),
        name="place",
    )(pick, pages)


def attend_kernel(width, q_ref, kv_ref, *refs):
    out_ref, list_ref, key_ref, value_ref, s_ref, acc_ref = refs[-6:]
    peers, span = kv_ref.shape[0], kv_ref.shape[1] // 2
    group, cap = q_ref.shape[0], q_ref.shape[1]

    @pl.when(pl.program_id(0) == 0)
    def _():
        there = [
            (jnp.max(kv_ref[src, :16, :].astype(F32)) < MARK / 2).astype(jnp.int32)
            for src in range(peers)
        ]
        count = jnp.int32(0)
        for src in range(peers):
            list_ref[count] = src
            count = count + there[src]
        list_ref[count] = list_ref[0]
        list_ref[peers + 1] = count
        even = ((count + 1) // 2) * 2

        def pack(n, carry):
            src = list_ref[n]
            at = pl.multiple_of(n * span, span)
            weight = jnp.where(n < count, 1.0, 0.0).astype(BF16)
            key_ref[pl.ds(at, span), :] = kv_ref[src, :span, :]
            value_ref[pl.ds(at, span), :HD] = kv_ref[src, span:, :] * weight
            value_ref[pl.ds(at, span), HD:] = jnp.full((span, HD), 1.0, BF16) * weight
            return carry

        lax.fori_loop(0, even, pack, 0)

    count = list_ref[peers + 1]
    even = ((count + 1) // 2) * 2
    heads = [(j, h) for j in range(group) for h in range(G)]
    q = jnp.concatenate([q_ref[j, :, h * HD : (h + 1) * HD] for j, h in heads], axis=0)
    fours = even // 4

    def score(at, size, top):
        key = key_ref[pl.ds(at, size), :]
        s = lax.dot_general(q, key, (((1,), (1,)), ((), ())), preferred_element_type=F32)
        s_ref[:, pl.ds(at, size)] = s
        for c in range(0, size, HD):
            top = jnp.maximum(top, s[:, c : c + HD])
        return top

    def four(i):
        return pl.multiple_of(i * 4 * span, 4 * span)

    def two(i):
        return pl.multiple_of(i * 2 * span, 2 * span)

    top = lax.fori_loop(
        0, fours, lambda i, t: score(four(i), 4 * span, t), jnp.full(q.shape, LOW, F32)
    )
    top = lax.fori_loop(2 * fours, even // 2, lambda i, t: score(two(i), 2 * span, t), top)
    top = jnp.max(top, axis=1, keepdims=True)
    acc_ref[...] = jnp.zeros_like(acc_ref)

    def weigh(at, size, carry):
        p = jnp.exp2((s_ref[:, pl.ds(at, size)] - top) * (SCALE * LOG2E)).astype(BF16)
        acc_ref[...] += jnp.dot(p, value_ref[pl.ds(at, size), :], preferred_element_type=F32)
        return carry

    lax.fori_loop(0, fours, lambda i, c: weigh(four(i), 4 * span, c), 0)
    lax.fori_loop(2 * fours, even // 2, lambda i, c: weigh(two(i), 2 * span, c), 0)
    total = acc_ref[:, HD:]
    total = jnp.where(total > 0.0, total, 1.0)
    out = (acc_ref[:, :HD] / total).astype(BF16)
    lane = lax.broadcasted_iota(jnp.int32, (cap, HD), 1)
    for j in range(group):
        packed_total = jnp.ones((cap, HD), F32)
        packed_top = jnp.zeros((cap, HD), F32)
        for h in range(G):
            at = (j * G + h) * cap
            out_ref[j, :, h * HD : (h + 1) * HD] = out[at : at + cap]
            packed_total = jnp.where((lane & 7) == h, total[at : at + cap], packed_total)
            packed_top = jnp.where((lane & 7) == h, top[at : at + cap], packed_top)
        lse = jnp.where(count > 0, packed_top * SCALE + jnp.log(packed_total), LOW)
        first = lse.astype(BF16).astype(F32)
        second = (lse - first).astype(BF16).astype(F32)
        third = lse - first - second
        part = jnp.where(lane < 8, first, jnp.where(lane < 16, second, third))
        out_ref[j, :, width:] = jnp.where(lane < 24, part, 0.0).astype(BF16)


def attend(q, kv, name, sub, begun=None):
    peers, rows, width = q.shape
    group = 8
    span = kv.shape[1] // 2
    m = group * CAP * G
    return pl.pallas_call(
        functools.partial(attend_kernel, width),
        grid=(peers // group,),
        out_shape=jax.ShapeDtypeStruct((peers, rows, width + HD), BF16),
        in_specs=[
            pl.BlockSpec((group, CAP, width), lambda i: (i, sub, 0)),
            pl.BlockSpec(memory_space=pltpu.VMEM),
        ]
        + [pl.BlockSpec(memory_space=pl.ANY)] * (begun is not None),
        out_specs=pl.BlockSpec((group, CAP, width + HD), lambda i: (i, sub, 0)),
        input_output_aliases={} if begun is None else {2: 0},
        scratch_shapes=[
            pltpu.SMEM((peers + 2,), jnp.int32),
            pltpu.VMEM((peers * span, HD), BF16),
            pltpu.VMEM((peers * span, 2 * HD), BF16),
            pltpu.VMEM((m, peers * span), F32),
            pltpu.VMEM((m, 2 * HD), F32),
        ],
        compiler_params=pltpu.CompilerParams(vmem_limit_bytes=32 * 2**20),
        cost_estimate=pl.CostEstimate(
            flops=4 * peers * CAP * G * peers * span * HD,
            bytes_accessed=32 * 2**20,
            transcendentals=peers * CAP * G * peers * span,
        ),
        name=name,
    )(*((q, kv) if begun is None else (q, kv, begun)))


def half_rows(rows, part):
    step = rows.shape[0] // 8
    half = step // 2
    return jnp.concatenate([rows[b * step + part * half : b * step + (part + 1) * half] for b in range(8)], axis=0)


def collect_kernel(col_ref, row_ref, replies_ref, low_ref, high_ref):
    slot = slots_as_col(col_ref[...], row_ref[...])
    n = slot.shape[0]
    pick = jnp.where(lax.broadcasted_iota(jnp.int32, (n, replies_ref.shape[0]), 1) == slot, 1.0, 0.0)
    rows = jnp.dot(pick.astype(BF16), replies_ref[...], preferred_element_type=F32).astype(BF16)
    low_ref[...] = half_rows(rows, 0)
    high_ref[...] = half_rows(rows, 1)


def collect(ids_col, ids_row, replies):
    n = ids_col.shape[0]
    return pl.pallas_call(
        collect_kernel,
        out_shape=(jax.ShapeDtypeStruct((n // 2, replies.shape[1]), BF16),) * 2,
        compiler_params=pltpu.CompilerParams(vmem_limit_bytes=32 * 2**20),
        cost_estimate=pl.CostEstimate(
            flops=2 * n * replies.shape[0] * replies.shape[1], bytes_accessed=2**21, transcendentals=0
        ),
        name="collect",
    )(ids_col, ids_row, replies)


def merge_kernel(part, me_ref, col_ref, row_ref, own_ref, far_ref, suf_ref, suf_lse_ref, w_ref, send_ref, keep_ref, att_ref, w_buf, sem):
    tile = w_ref.shape[1] // sem.shape[0]
    fetches = [
        pltpu.make_async_copy(
            w_ref.at[:, pl.ds(t * tile, tile)], w_buf.at[:, pl.ds(t * tile, tile)], sem.at[t]
        )
        for t in range(sem.shape[0])
    ]
    for fetch in fetches:
        fetch.start()
    n, width = suf_ref.shape
    slot = slots_as_col(col_ref[...], row_ref[...])
    pick = jnp.where(lax.broadcasted_iota(jnp.int32, (n, own_ref.shape[0]), 1) == slot, 1.0, 0.0)
    pick = half_rows(pick.astype(BF16), part)
    own = jnp.dot(pick, own_ref[...], preferred_element_type=F32)
    far = far_ref[...]
    i = lax.broadcasted_iota(jnp.int32, (HD, width), 0)
    c = lax.broadcasted_iota(jnp.int32, (HD, width), 1)
    spread = jnp.where((i < 24) & ((i & 7) == (c >> 7)), 1.0, 0.0).astype(BF16)
    own_lse = jnp.dot(own[:, width:].astype(BF16), spread, preferred_element_type=F32)
    far_lse = jnp.dot(far[:, width:], spread, preferred_element_type=F32)
    suf_lse = half_rows(suf_lse_ref, part)
    top = jnp.maximum(jnp.maximum(own_lse, far_lse), suf_lse)
    a = jnp.exp(own_lse - top)
    b = jnp.exp(far_lse - top)
    s = jnp.exp(suf_lse - top)
    att = a * own[:, :width] + b * far[:, :width].astype(F32) + s * half_rows(suf_ref, part)
    att_ref[0] = (att / (a + b + s)).astype(BF16)
    me = me_ref[0]
    step = att_ref.shape[1] // 8
    for q in range(8):
        flip = (1 - q // 4) + 2 * (1 - (q // 2) % 2) + 4 * (1 - q % 2)
        at = pl.multiple_of((me ^ flip) * step, step)
        att_ref[1, q * step : (q + 1) * step] = att_ref[0, pl.ds(at, step), :]
    half = send_ref.shape[0]
    for t, fetch in enumerate(fetches):
        fetch.wait()
        out = jnp.dot(
            att_ref[1], w_buf[:, t * tile : (t + 1) * tile], preferred_element_type=F32
        ).astype(BF16)
        send_ref[:, t * tile : (t + 1) * tile] = out[:half]
        keep_ref[:, t * tile : (t + 1) * tile] = out[half:]


def merge_project(part, me, ids_col, ids_row, own, far, suf, suf_lse, weight):
    n, width = suf.shape
    columns = weight.shape[1]
    whole = pl.BlockSpec(memory_space=pltpu.VMEM)
    shape = jax.ShapeDtypeStruct((n // 4, columns), BF16)
    return pl.pallas_call(
        functools.partial(merge_kernel, part),
        out_shape=(shape, shape),
        in_specs=[pl.BlockSpec(memory_space=pltpu.SMEM)]
        + [whole] * 6
        + [pl.BlockSpec(memory_space=pl.ANY)],
        out_specs=(whole, whole),
        scratch_shapes=[
            pltpu.VMEM((2, n // 2, width), BF16),
            pltpu.VMEM((width, columns), BF16),
            pltpu.SemaphoreType.DMA((8,)),
        ],
        compiler_params=pltpu.CompilerParams(vmem_limit_bytes=56 * 2**20),
        cost_estimate=pl.CostEstimate(
            flops=8 * n * width * columns, bytes_accessed=24 * 2**20, transcendentals=2 * n * width
        ),
        name="merge_project",
    )(me, ids_col, ids_row, own, far, suf, suf_lse, weight)


def suffix_attend(queries, suffix_cache, suffix_len):
    seq, width = queries.shape
    rows = suffix_cache.shape[1]
    heads = queries.reshape(seq, width // HD, HD)
    scores = (
        jnp.einsum("sgd,std->sgt", heads, suffix_cache[:, :, 0], preferred_element_type=F32) * SCALE
    )
    in_length = (jnp.arange(rows, dtype=jnp.int32)[None, :] < suffix_len[:, None])[:, None, :]
    scores = jnp.where(in_length, scores, LOW)
    highest = jnp.max(scores, axis=-1)
    exp_terms = jnp.where(in_length, jnp.exp(scores - highest[..., None]), 0.0)
    totals = jnp.sum(exp_terms, axis=-1)
    out = (
        jnp.einsum("sgt,std->sgd", exp_terms.astype(BF16), suffix_cache[:, :, 1], preferred_element_type=F32)
        / totals[..., None]
    )
    lse = jnp.broadcast_to((highest + jnp.log(totals))[..., None], out.shape)
    return out.reshape(seq, width), lse.reshape(seq, width)


def swap(value, axis, bit):
    size = lax.axis_size(axis)
    return lax.ppermute(value, axis, [(i, i ^ bit) for i in range(size)])


def local(prefill_pages, page_owner, queries, suffix_cache, suffix_len, prefix_id, out_weight):
    plane = lax.axis_size("x") * lax.axis_size("y")
    pages, page = prefill_pages.shape[:2]
    seq, width = queries.shape
    pairs = pages // 2
    ids_col, ids_row = prefix_id, prefix_id.reshape(1, seq)
    far_row = swap(ids_row, "zh", 1)

    sent = dispatch(ids_col, ids_row, queries, plane * 2 * CAP).reshape(plane, 2 * CAP, width)
    own_q = lax.all_to_all(sent, PLANE, 0, 0, tiled=True)

    owner = page_owner[0, ::2]
    slot = slot_base(owner) // CAP
    here = jnp.arange(2 * plane, dtype=jnp.int32)[:, None] == slot[None, :]
    pick = jnp.sum(jnp.where(here, jnp.arange(pairs, dtype=jnp.int32)[None, :] + 1, 0), axis=1) - 1
    paired = jnp.swapaxes(prefill_pages.reshape(pairs, 2 * page, 2, HD), 1, 2)
    paired = paired.reshape(pairs, 4 * page, HD)
    first, second = place(pick, paired, plane)
    first, second, own_q, far_row = lax.optimization_barrier((first, second, own_q, far_row))
    far_col = far_row.reshape(seq, 1)
    far_q = swap(own_q, "zh", 1)
    first = lax.all_to_all(first, PLANE, 0, 0, tiled=True)
    first, second = lax.optimization_barrier((first, second))
    second = lax.all_to_all(second, PLANE, 0, 0, tiled=True)
    own_out = attend(own_q, first, "attend_own", 0)
    own_out, later, suffix_cache = lax.optimization_barrier((own_out, queries, suffix_cache))
    suf, suf_lse = suffix_attend(later, suffix_cache, suffix_len)
    far_q, own_out, suf, suf_lse = lax.optimization_barrier((far_q, own_out, suf, suf_lse))
    far_out = attend(far_q, first, "attend_far", 0)
    far_out = attend(far_q, second, "attend_far", 1, far_out)
    far_out, own_q = lax.optimization_barrier((far_out, own_q))
    far_back = lax.all_to_all(far_out, PLANE, 0, 0, tiled=True)
    own_out = attend(own_q, second, "attend_own", 1, own_out)
    far_back, own_out = lax.optimization_barrier((far_back, own_out))
    far_part = collect(far_col, far_row, far_back.reshape(plane * 2 * CAP, width + HD))
    far_part, own_out = lax.optimization_barrier((far_part, own_out))
    far_low = swap(far_part[0], "zh", 1)
    far_high = swap(far_part[1], "zh", 1)
    own_back = lax.all_to_all(own_out, PLANE, 0, 0, tiled=True)

    me = (lax.axis_index("zl") * 2 + lax.axis_index("core")).astype(jnp.int32).reshape(1)
    own_back = own_back.reshape(plane * 2 * CAP, width + HD)
    halves = [
        merge_project(part, me, ids_col, ids_row, own_back, far, suf, suf_lse, out_weight)
        for part, far in enumerate((far_low, far_high))
    ]

    def add(a, b):
        return (a.astype(F32) + b.astype(F32)).astype(BF16)

    def fold(send, keep, axis, bit):
        got = swap(send, axis, bit)
        half = keep.shape[0] // 2
        return add(keep[:half], got[:half]), add(keep[half:], got[half:])

    halves = [fold(send, keep, "core", 1) for send, keep in halves]
    halves = [fold(send, keep, "zl", 1) for send, keep in halves]
    return jnp.concatenate([add(keep, swap(send, "zl", 2)) for send, keep in halves], axis=0)


def solution(mesh):
    x, zh, y, zl, core = 4, 2, 4, 4, 2
    names = ("x", "zh", "y", "zl", "core")
    fine = Mesh(mesh.devices.reshape(x, zh, y, zl, core), names)
    pool, tp = ("x", "zh", "y"), ("zl", "core")
    in_specs = (
        P(pool, None, None, tp),
        P(pool, None),
        P(pool, tp),
        P(pool, None, None, tp),
        P(pool),
        P(pool, None),
        P(tp, None),
    )
    out_specs = P(pool + tp, None)
    return jax.shard_map(local, mesh=fine, in_specs=in_specs, out_specs=out_specs, check_vma=False)
```

```python
import functools

import jax
import jax.numpy as jnp
from jax import lax
from jax.experimental import pallas as pl
from jax.experimental.pallas import tpu as pltpu
from jax.sharding import Mesh
from jax.sharding import PartitionSpec as P

HD = 128
G = 8
CAP = 16
PLANE = ("x", "y")
SCALE = HD**-0.5
LOG2E = 1.4426950408889634
LOW = -1e30
MARK = 16384.0
F32 = jnp.float32
BF16 = jnp.bfloat16


def slot_base(ids):
    return (((ids >> 3) * 4 + (ids & 3)) * 2 + ((ids >> 2) & 1)) * CAP


def slots_as_col(ids_col, ids_row):
    n = ids_row.shape[1]
    i = lax.broadcasted_iota(jnp.int32, (n, n), 0)
    j = lax.broadcasted_iota(jnp.int32, (n, n), 1)
    earlier = jnp.where((ids_col == ids_row) & (j < i), 1.0, 0.0)
    rank = jnp.sum(earlier, axis=1, keepdims=True).astype(jnp.int32)
    return slot_base(ids_col) + rank


def dispatch_kernel(row_ref, q_ref, out_ref):
    ids = row_ref[...]
    rows, n = out_ref.shape[0], ids.shape[1]
    named = lax.broadcasted_iota(jnp.int32, (rows // CAP, n), 0) == ids
    i = lax.broadcasted_iota(jnp.int32, (n, n), 0)
    j = lax.broadcasted_iota(jnp.int32, (n, n), 1)
    ahead = jnp.where(i < j, 1.0, 0.0).astype(BF16)
    earlier = jnp.dot(jnp.where(named, 1.0, 0.0).astype(BF16), ahead, preferred_element_type=F32)
    rank = jnp.sum(jnp.where(named, earlier, 0.0), axis=0, keepdims=True).astype(jnp.int32)
    slot = slot_base(ids) + rank
    pick = jnp.where(lax.broadcasted_iota(jnp.int32, (rows, n), 0) == slot, 1.0, 0.0)
    out_ref[...] = jnp.dot(pick.astype(BF16), q_ref[...], preferred_element_type=F32).astype(BF16)


def dispatch(ids_row, queries, rows):
    return pl.pallas_call(
        dispatch_kernel,
        out_shape=jax.ShapeDtypeStruct((rows, queries.shape[1]), BF16),
        compiler_params=pltpu.CompilerParams(vmem_limit_bytes=32 * 2**20),
        cost_estimate=pl.CostEstimate(
            flops=2 * rows * queries.shape[0] * queries.shape[1], bytes_accessed=2**21, transcendentals=0
        ),
        name="dispatch",
    )(ids_row, queries)


def place_kernel(pick_ref, pages_ref, *out_refs):
    for sub, out_ref in enumerate(out_refs):

        def one(group, carry):
            src = pick_ref[2 * group + sub]
            out_ref[group] = pages_ref[jnp.maximum(src, 0)]

            @pl.when(src < 0)
            def _():
                out_ref[group, :16, :] = jnp.full((16, HD), MARK, BF16)

            return carry

        lax.fori_loop(0, out_ref.shape[0], one, 0)


def place(pick, pages, plane):
    whole = pl.BlockSpec(memory_space=pltpu.VMEM)
    return pl.pallas_call(
        place_kernel,
        out_shape=(jax.ShapeDtypeStruct((plane,) + pages.shape[1:], BF16),) * 2,
        in_specs=[pl.BlockSpec(memory_space=pltpu.SMEM), whole],
        out_specs=(whole, whole),
        compiler_params=pltpu.CompilerParams(vmem_limit_bytes=32 * 2**20),
        cost_estimate=pl.CostEstimate(flops=0, bytes_accessed=6 * 2**20, transcendentals=0),
        name="place",
    )(pick, pages)


def attend_kernel(width, q_ref, kv_ref, *refs):
    out_ref, list_ref, key_ref, value_ref, s_ref, acc_ref = refs[-6:]
    peers, span = kv_ref.shape[0], kv_ref.shape[1] // 2
    group, cap = q_ref.shape[0], q_ref.shape[1]

    @pl.when(pl.program_id(0) == 0)
    def _():
        there = [
            (jnp.max(kv_ref[src, :16, :].astype(F32)) < MARK / 2).astype(jnp.int32)
            for src in range(peers)
        ]
        count = jnp.int32(0)
        for src in range(peers):
            list_ref[count] = src
            count = count + there[src]
        list_ref[count] = list_ref[0]
        list_ref[peers + 1] = count
        even = ((count + 1) // 2) * 2

        def pack(n, carry):
            src = list_ref[n]
            at = pl.multiple_of(n * span, span)
            weight = jnp.where(n < count, 1.0, 0.0).astype(BF16)
            key_ref[pl.ds(at, span), :] = kv_ref[src, :span, :]
            value_ref[pl.ds(at, span), :HD] = kv_ref[src, span:, :] * weight
            value_ref[pl.ds(at, span), HD:] = jnp.full((span, HD), 1.0, BF16) * weight
            return carry

        lax.fori_loop(0, even, pack, 0)

    count = list_ref[peers + 1]
    even = ((count + 1) // 2) * 2
    heads = [(j, h) for j in range(group) for h in range(G)]
    q = jnp.concatenate([q_ref[j, :, h * HD : (h + 1) * HD] for j, h in heads], axis=0)
    fours = even // 4

    def score(at, size, top):
        key = key_ref[pl.ds(at, size), :]
        s = lax.dot_general(q, key, (((1,), (1,)), ((), ())), preferred_element_type=F32)
        s_ref[:, pl.ds(at, size)] = s
        for c in range(0, size, HD):
            top = jnp.maximum(top, s[:, c : c + HD])
        return top

    def four(i):
        return pl.multiple_of(i * 4 * span, 4 * span)

    def two(i):
        return pl.multiple_of(i * 2 * span, 2 * span)

    top = lax.fori_loop(
        0, fours, lambda i, t: score(four(i), 4 * span, t), jnp.full(q.shape, LOW, F32)
    )
    top = lax.fori_loop(2 * fours, even // 2, lambda i, t: score(two(i), 2 * span, t), top)
    top = jnp.max(top, axis=1, keepdims=True)
    acc_ref[...] = jnp.zeros_like(acc_ref)

    def weigh(at, size, carry):
        p = jnp.exp2((s_ref[:, pl.ds(at, size)] - top) * (SCALE * LOG2E)).astype(BF16)
        acc_ref[...] += jnp.dot(p, value_ref[pl.ds(at, size), :], preferred_element_type=F32)
        return carry

    lax.fori_loop(0, fours, lambda i, c: weigh(four(i), 4 * span, c), 0)
    lax.fori_loop(2 * fours, even // 2, lambda i, c: weigh(two(i), 2 * span, c), 0)
    total = acc_ref[:, HD:]
    total = jnp.where(total > 0.0, total, 1.0)
    out = (acc_ref[:, :HD] / total).astype(BF16)
    lane = lax.broadcasted_iota(jnp.int32, (cap, HD), 1)
    for j in range(group):
        packed_total = jnp.ones((cap, HD), F32)
        packed_top = jnp.zeros((cap, HD), F32)
        for h in range(G):
            at = (j * G + h) * cap
            out_ref[j, :, h * HD : (h + 1) * HD] = out[at : at + cap]
            packed_total = jnp.where((lane & 7) == h, total[at : at + cap], packed_total)
            packed_top = jnp.where((lane & 7) == h, top[at : at + cap], packed_top)
        lse = jnp.where(count > 0, packed_top * SCALE + jnp.log(packed_total), LOW)
        first = lse.astype(BF16).astype(F32)
        second = (lse - first).astype(BF16).astype(F32)
        third = lse - first - second
        part = jnp.where(lane < 8, first, jnp.where(lane < 16, second, third))
        out_ref[j, :, width:] = jnp.where(lane < 24, part, 0.0).astype(BF16)


def attend(q, kv, name, sub, begun=None):
    peers, rows, width = q.shape
    group = 8
    span = kv.shape[1] // 2
    m = group * CAP * G
    return pl.pallas_call(
        functools.partial(attend_kernel, width),
        grid=(peers // group,),
        out_shape=jax.ShapeDtypeStruct((peers, rows, width + HD), BF16),
        in_specs=[
            pl.BlockSpec((group, CAP, width), lambda i: (i, sub, 0)),
            pl.BlockSpec(memory_space=pltpu.VMEM),
        ]
        + [pl.BlockSpec(memory_space=pl.ANY)] * (begun is not None),
        out_specs=pl.BlockSpec((group, CAP, width + HD), lambda i: (i, sub, 0)),
        input_output_aliases={} if begun is None else {2: 0},
        scratch_shapes=[
            pltpu.SMEM((peers + 2,), jnp.int32),
            pltpu.VMEM((peers * span, HD), BF16),
            pltpu.VMEM((peers * span, 2 * HD), BF16),
            pltpu.VMEM((m, peers * span), F32),
            pltpu.VMEM((m, 2 * HD), F32),
        ],
        compiler_params=pltpu.CompilerParams(vmem_limit_bytes=32 * 2**20),
        cost_estimate=pl.CostEstimate(
            flops=4 * peers * CAP * G * peers * span * HD,
            bytes_accessed=32 * 2**20,
            transcendentals=peers * CAP * G * peers * span,
        ),
        name=name,
    )(*((q, kv) if begun is None else (q, kv, begun)))


def half_rows(rows, part):
    step = rows.shape[0] // 8
    half = step // 2
    return jnp.concatenate([rows[b * step + part * half : b * step + (part + 1) * half] for b in range(8)], axis=0)


def collect_kernel(col_ref, row_ref, replies_ref, low_ref, high_ref):
    slot = slots_as_col(col_ref[...], row_ref[...])
    n = slot.shape[0]
    pick = jnp.where(lax.broadcasted_iota(jnp.int32, (n, replies_ref.shape[0]), 1) == slot, 1.0, 0.0)
    rows = jnp.dot(pick.astype(BF16), replies_ref[...], preferred_element_type=F32).astype(BF16)
    low_ref[...] = half_rows(rows, 0)
    high_ref[...] = half_rows(rows, 1)


def collect(ids_col, ids_row, replies):
    n = ids_col.shape[0]
    return pl.pallas_call(
        collect_kernel,
        out_shape=(jax.ShapeDtypeStruct((n // 2, replies.shape[1]), BF16),) * 2,
        compiler_params=pltpu.CompilerParams(vmem_limit_bytes=32 * 2**20),
        cost_estimate=pl.CostEstimate(
            flops=2 * n * replies.shape[0] * replies.shape[1], bytes_accessed=2**21, transcendentals=0
        ),
        name="collect",
    )(ids_col, ids_row, replies)


def merge_kernel(part, me_ref, col_ref, row_ref, own_ref, far_ref, suf_ref, suf_lse_ref, w_ref, send_ref, keep_ref, att_ref, w_buf, sem):
    tile = w_ref.shape[1] // sem.shape[0]
    fetches = [
        pltpu.make_async_copy(
            w_ref.at[:, pl.ds(t * tile, tile)], w_buf.at[:, pl.ds(t * tile, tile)], sem.at[t]
        )
        for t in range(sem.shape[0])
    ]
    for fetch in fetches:
        fetch.start()
    n, width = suf_ref.shape
    slot = slots_as_col(col_ref[...], row_ref[...])
    pick = jnp.where(lax.broadcasted_iota(jnp.int32, (n, own_ref.shape[0]), 1) == slot, 1.0, 0.0)
    pick = half_rows(pick.astype(BF16), part)
    own = jnp.dot(pick, own_ref[...], preferred_element_type=F32)
    far = far_ref[...]
    i = lax.broadcasted_iota(jnp.int32, (HD, width), 0)
    c = lax.broadcasted_iota(jnp.int32, (HD, width), 1)
    spread = jnp.where((i < 24) & ((i & 7) == (c >> 7)), 1.0, 0.0).astype(BF16)
    own_lse = jnp.dot(own[:, width:].astype(BF16), spread, preferred_element_type=F32)
    far_lse = jnp.dot(far[:, width:], spread, preferred_element_type=F32)
    suf_lse = half_rows(suf_lse_ref, part)
    top = jnp.maximum(jnp.maximum(own_lse, far_lse), suf_lse)
    a = jnp.exp(own_lse - top)
    b = jnp.exp(far_lse - top)
    s = jnp.exp(suf_lse - top)
    att = a * own[:, :width] + b * far[:, :width].astype(F32) + s * half_rows(suf_ref, part)
    att_ref[0] = (att / (a + b + s)).astype(BF16)
    me = me_ref[0]
    step = att_ref.shape[1] // 8
    for q in range(8):
        flip = (1 - q // 4) + 2 * (1 - (q // 2) % 2) + 4 * (1 - q % 2)
        at = pl.multiple_of((me ^ flip) * step, step)
        att_ref[1, q * step : (q + 1) * step] = att_ref[0, pl.ds(at, step), :]
    half = send_ref.shape[0]
    for t, fetch in enumerate(fetches):
        fetch.wait()
        out = jnp.dot(
            att_ref[1], w_buf[:, t * tile : (t + 1) * tile], preferred_element_type=F32
        ).astype(BF16)
        send_ref[:, t * tile : (t + 1) * tile] = out[:half]
        keep_ref[:, t * tile : (t + 1) * tile] = out[half:]


def merge_project(part, me, ids_col, ids_row, own, far, suf, suf_lse, weight):
    n, width = suf.shape
    columns = weight.shape[1]
    whole = pl.BlockSpec(memory_space=pltpu.VMEM)
    shape = jax.ShapeDtypeStruct((n // 4, columns), BF16)
    return pl.pallas_call(
        functools.partial(merge_kernel, part),
        out_shape=(shape, shape),
        in_specs=[pl.BlockSpec(memory_space=pltpu.SMEM)]
        + [whole] * 6
        + [pl.BlockSpec(memory_space=pl.ANY)],
        out_specs=(whole, whole),
        scratch_shapes=[
            pltpu.VMEM((2, n // 2, width), BF16),
            pltpu.VMEM((width, columns), BF16),
            pltpu.SemaphoreType.DMA((8,)),
        ],
        compiler_params=pltpu.CompilerParams(vmem_limit_bytes=56 * 2**20),
        cost_estimate=pl.CostEstimate(
            flops=8 * n * width * columns, bytes_accessed=24 * 2**20, transcendentals=2 * n * width
        ),
        name="merge_project",
    )(me, ids_col, ids_row, own, far, suf, suf_lse, weight)


def suffix_attend(queries, suffix_cache, suffix_len):
    seq, width = queries.shape
    rows = suffix_cache.shape[1]
    heads = queries.reshape(seq, width // HD, HD)
    scores = (
        jnp.einsum("sgd,std->sgt", heads, suffix_cache[:, :, 0], preferred_element_type=F32) * SCALE
    )
    in_length = (jnp.arange(rows, dtype=jnp.int32)[None, :] < suffix_len[:, None])[:, None, :]
    scores = jnp.where(in_length, scores, LOW)
    highest = jnp.max(scores, axis=-1)
    exp_terms = jnp.where(in_length, jnp.exp(scores - highest[..., None]), 0.0)
    totals = jnp.sum(exp_terms, axis=-1)
    out = (
        jnp.einsum("sgt,std->sgd", exp_terms.astype(BF16), suffix_cache[:, :, 1], preferred_element_type=F32)
        / totals[..., None]
    )
    lse = jnp.broadcast_to((highest + jnp.log(totals))[..., None], out.shape)
    return out.reshape(seq, width), lse.reshape(seq, width)


def swap(value, axis, bit):
    size = lax.axis_size(axis)
    return lax.ppermute(value, axis, [(i, i ^ bit) for i in range(size)])


def local(prefill_pages, page_owner, queries, suffix_cache, suffix_len, prefix_id, out_weight):
    plane = lax.axis_size("x") * lax.axis_size("y")
    pages, page = prefill_pages.shape[:2]
    seq, width = queries.shape
    pairs = pages // 2
    ids_col, ids_row = prefix_id, prefix_id.reshape(1, seq)
    far_row = swap(ids_row, "zh", 1)

    sent = dispatch(ids_row, queries, plane * 2 * CAP).reshape(plane, 2 * CAP, width)
    own_q = lax.all_to_all(sent, PLANE, 0, 0, tiled=True)

    owner = page_owner[0, ::2]
    slot = slot_base(owner) // CAP
    here = jnp.arange(2 * plane, dtype=jnp.int32)[:, None] == slot[None, :]
    pick = jnp.sum(jnp.where(here, jnp.arange(pairs, dtype=jnp.int32)[None, :] + 1, 0), axis=1) - 1
    paired = jnp.swapaxes(prefill_pages.reshape(pairs, 2 * page, 2, HD), 1, 2)
    paired = paired.reshape(pairs, 4 * page, HD)
    first, second = place(pick, paired, plane)
    first, second, own_q, far_row = lax.optimization_barrier((first, second, own_q, far_row))
    far_col = far_row.reshape(seq, 1)
    far_q = swap(own_q, "zh", 1)
    first = lax.all_to_all(first, PLANE, 0, 0, tiled=True)
    first, second = lax.optimization_barrier((first, second))
    second = lax.all_to_all(second, PLANE, 0, 0, tiled=True)
    own_out = attend(own_q, first, "attend_own", 0)
    own_out, later, suffix_cache = lax.optimization_barrier((own_out, queries, suffix_cache))
    suf, suf_lse = suffix_attend(later, suffix_cache, suffix_len)
    far_q, own_out, suf, suf_lse = lax.optimization_barrier((far_q, own_out, suf, suf_lse))
    far_out = attend(far_q, first, "attend_far", 0)
    far_out = attend(far_q, second, "attend_far", 1, far_out)
    far_out, own_q = lax.optimization_barrier((far_out, own_q))
    far_back = lax.all_to_all(far_out, PLANE, 0, 0, tiled=True)
    own_out = attend(own_q, second, "attend_own", 1, own_out)
    far_back, own_out = lax.optimization_barrier((far_back, own_out))
    far_part = collect(far_col, far_row, far_back.reshape(plane * 2 * CAP, width + HD))
    far_part, own_out = lax.optimization_barrier((far_part, own_out))
    far_low = swap(far_part[0], "zh", 1)
    far_high = swap(far_part[1], "zh", 1)
    own_back = lax.all_to_all(own_out, PLANE, 0, 0, tiled=True)

    me = (lax.axis_index("zl") * 2 + lax.axis_index("core")).astype(jnp.int32).reshape(1)
    own_back = own_back.reshape(plane * 2 * CAP, width + HD)
    halves = [
        merge_project(part, me, ids_col, ids_row, own_back, far, suf, suf_lse, out_weight)
        for part, far in enumerate((far_low, far_high))
    ]

    def add(a, b):
        return (a.astype(F32) + b.astype(F32)).astype(BF16)

    def spread(send, keep):
        got = swap(send, "core", 1)
        step = keep.shape[0] // 4
        blocks = [add(keep[q * step : (q + 1) * step], got[q * step : (q + 1) * step]) for q in range(4)]
        parts = [swap(blocks[q], "zl", bit) for q, bit in ((0, 3), (2, 2), (1, 1))]
        total = blocks[3].astype(F32)
        for part in parts:
            total = total + part.astype(F32)
        return total.astype(BF16)

    return jnp.concatenate([spread(*half) for half in halves], axis=0)


def solution(mesh):
    x, zh, y, zl, core = 4, 2, 4, 4, 2
    names = ("x", "zh", "y", "zl", "core")
    fine = Mesh(mesh.devices.reshape(x, zh, y, zl, core), names)
    pool, tp = ("x", "zh", "y"), ("zl", "core")
    in_specs = (
        P(pool, None, None, tp),
        P(pool, None),
        P(pool, tp),
        P(pool, None, None, tp),
        P(pool),
        P(pool, None),
        P(tp, None),
    )
    out_specs = P(pool + tp, None)
    return jax.shard_map(local, mesh=fine, in_specs=in_specs, out_specs=out_specs, check_vma=False)
```

```python
import functools

import jax
import jax.numpy as jnp
from jax import lax
from jax.experimental import pallas as pl
from jax.experimental.pallas import tpu as pltpu
from jax.sharding import Mesh
from jax.sharding import PartitionSpec as P

HD = 128
G = 8
CAP = 16
PLANE = ("x", "y")
SCALE = HD**-0.5
LOG2E = 1.4426950408889634
LOW = -1e30
MARK = 16384.0
F32 = jnp.float32
BF16 = jnp.bfloat16


def slot_base(ids):
    return (((ids >> 3) * 4 + (ids & 3)) * 2 + ((ids >> 2) & 1)) * CAP


def slots_as_col(ids_col, ids_row):
    n = ids_row.shape[1]
    i = lax.broadcasted_iota(jnp.int32, (n, n), 0)
    j = lax.broadcasted_iota(jnp.int32, (n, n), 1)
    earlier = jnp.where((ids_col == ids_row) & (j < i), 1.0, 0.0)
    rank = jnp.sum(earlier, axis=1, keepdims=True).astype(jnp.int32)
    return slot_base(ids_col) + rank


def dispatch_kernel(row_ref, q_ref, out_ref):
    ids = row_ref[...]
    rows, n = out_ref.shape[0], ids.shape[1]
    named = lax.broadcasted_iota(jnp.int32, (rows // CAP, n), 0) == ids
    i = lax.broadcasted_iota(jnp.int32, (n, n), 0)
    j = lax.broadcasted_iota(jnp.int32, (n, n), 1)
    ahead = jnp.where(i < j, 1.0, 0.0).astype(BF16)
    earlier = jnp.dot(jnp.where(named, 1.0, 0.0).astype(BF16), ahead, preferred_element_type=F32)
    rank = jnp.sum(jnp.where(named, earlier, 0.0), axis=0, keepdims=True).astype(jnp.int32)
    slot = slot_base(ids) + rank
    pick = jnp.where(lax.broadcasted_iota(jnp.int32, (rows, n), 0) == slot, 1.0, 0.0)
    out_ref[...] = jnp.dot(pick.astype(BF16), q_ref[...], preferred_element_type=F32).astype(BF16)


def dispatch(ids_row, queries, rows):
    return pl.pallas_call(
        dispatch_kernel,
        out_shape=jax.ShapeDtypeStruct((rows, queries.shape[1]), BF16),
        compiler_params=pltpu.CompilerParams(vmem_limit_bytes=32 * 2**20),
        cost_estimate=pl.CostEstimate(
            flops=2 * rows * queries.shape[0] * queries.shape[1], bytes_accessed=2**21, transcendentals=0
        ),
        name="dispatch",
    )(ids_row, queries)


def place_kernel(pick_ref, pages_ref, *out_refs):
    for sub, out_ref in enumerate(out_refs):

        def one(group, carry):
            src = pick_ref[2 * group + sub]
            out_ref[group] = pages_ref[jnp.maximum(src, 0)]

            @pl.when(src < 0)
            def _():
                out_ref[group, :16, :] = jnp.full((16, HD), MARK, BF16)

            return carry

        lax.fori_loop(0, out_ref.shape[0], one, 0)


def place(pick, pages, plane):
    whole = pl.BlockSpec(memory_space=pltpu.VMEM)
    return pl.pallas_call(
        place_kernel,
        out_shape=(jax.ShapeDtypeStruct((plane,) + pages.shape[1:], BF16),) * 2,
        in_specs=[pl.BlockSpec(memory_space=pltpu.SMEM), whole],
        out_specs=(whole, whole),
        compiler_params=pltpu.CompilerParams(vmem_limit_bytes=32 * 2**20),
        cost_estimate=pl.CostEstimate(flops=0, bytes_accessed=6 * 2**20, transcendentals=0),
        name="place",
    )(pick, pages)


def attend_kernel(width, q_ref, kv_ref, *refs):
    out_ref, list_ref, key_ref, value_ref, s_ref, acc_ref = refs[-6:]
    peers, span = kv_ref.shape[0], kv_ref.shape[1] // 2
    group, cap = q_ref.shape[0], q_ref.shape[1]

    @pl.when(pl.program_id(0) == 0)
    def _():
        there = [
            (jnp.max(kv_ref[src, :16, :].astype(F32)) < MARK / 2).astype(jnp.int32)
            for src in range(peers)
        ]
        count = jnp.int32(0)
        for src in range(peers):
            list_ref[count] = src
            count = count + there[src]
        list_ref[count] = list_ref[0]
        list_ref[peers + 1] = count
        even = ((count + 1) // 2) * 2

        def pack(n, carry):
            src = list_ref[n]
            at = pl.multiple_of(n * span, span)
            weight = jnp.where(n < count, 1.0, 0.0).astype(BF16)
            key_ref[pl.ds(at, span), :] = kv_ref[src, :span, :]
            value_ref[pl.ds(at, span), :HD] = kv_ref[src, span:, :] * weight
            value_ref[pl.ds(at, span), HD:] = jnp.full((span, HD), 1.0, BF16) * weight
            return carry

        lax.fori_loop(0, even, pack, 0)

    count = list_ref[peers + 1]
    even = ((count + 1) // 2) * 2
    heads = [(j, h) for j in range(group) for h in range(G)]
    q = jnp.concatenate([q_ref[j, :, h * HD : (h + 1) * HD] for j, h in heads], axis=0)
    fours = even // 4

    def score(at, size, top):
        key = key_ref[pl.ds(at, size), :]
        s = lax.dot_general(q, key, (((1,), (1,)), ((), ())), preferred_element_type=F32)
        s_ref[:, pl.ds(at, size)] = s
        for c in range(0, size, HD):
            top = jnp.maximum(top, s[:, c : c + HD])
        return top

    def four(i):
        return pl.multiple_of(i * 4 * span, 4 * span)

    def two(i):
        return pl.multiple_of(i * 2 * span, 2 * span)

    top = lax.fori_loop(
        0, fours, lambda i, t: score(four(i), 4 * span, t), jnp.full(q.shape, LOW, F32)
    )
    top = lax.fori_loop(2 * fours, even // 2, lambda i, t: score(two(i), 2 * span, t), top)
    top = jnp.max(top, axis=1, keepdims=True)
    acc_ref[...] = jnp.zeros_like(acc_ref)

    def weigh(at, size, carry):
        p = jnp.exp2((s_ref[:, pl.ds(at, size)] - top) * (SCALE * LOG2E)).astype(BF16)
        acc_ref[...] += jnp.dot(p, value_ref[pl.ds(at, size), :], preferred_element_type=F32)
        return carry

    lax.fori_loop(0, fours, lambda i, c: weigh(four(i), 4 * span, c), 0)
    lax.fori_loop(2 * fours, even // 2, lambda i, c: weigh(two(i), 2 * span, c), 0)
    total = acc_ref[:, HD:]
    total = jnp.where(total > 0.0, total, 1.0)
    out = (acc_ref[:, :HD] / total).astype(BF16)
    lane = lax.broadcasted_iota(jnp.int32, (cap, HD), 1)
    for j in range(group):
        packed_total = jnp.ones((cap, HD), F32)
        packed_top = jnp.zeros((cap, HD), F32)
        for h in range(G):
            at = (j * G + h) * cap
            out_ref[j, :, h * HD : (h + 1) * HD] = out[at : at + cap]
            packed_total = jnp.where((lane & 7) == h, total[at : at + cap], packed_total)
            packed_top = jnp.where((lane & 7) == h, top[at : at + cap], packed_top)
        lse = jnp.where(count > 0, packed_top * SCALE + jnp.log(packed_total), LOW)
        first = lse.astype(BF16).astype(F32)
        second = (lse - first).astype(BF16).astype(F32)
        third = lse - first - second
        part = jnp.where(lane < 8, first, jnp.where(lane < 16, second, third))
        out_ref[j, :, width:] = jnp.where(lane < 24, part, 0.0).astype(BF16)


def attend(q, kv, name, sub, begun=None):
    peers, rows, width = q.shape
    group = 8
    span = kv.shape[1] // 2
    m = group * CAP * G
    return pl.pallas_call(
        functools.partial(attend_kernel, width),
        grid=(peers // group,),
        out_shape=jax.ShapeDtypeStruct((peers, rows, width + HD), BF16),
        in_specs=[
            pl.BlockSpec((group, CAP, width), lambda i: (i, sub, 0)),
            pl.BlockSpec(memory_space=pltpu.VMEM),
        ]
        + [pl.BlockSpec(memory_space=pl.ANY)] * (begun is not None),
        out_specs=pl.BlockSpec((group, CAP, width + HD), lambda i: (i, sub, 0)),
        input_output_aliases={} if begun is None else {2: 0},
        scratch_shapes=[
            pltpu.SMEM((peers + 2,), jnp.int32),
            pltpu.VMEM((peers * span, HD), BF16),
            pltpu.VMEM((peers * span, 2 * HD), BF16),
            pltpu.VMEM((m, peers * span), F32),
            pltpu.VMEM((m, 2 * HD), F32),
        ],
        compiler_params=pltpu.CompilerParams(vmem_limit_bytes=32 * 2**20),
        cost_estimate=pl.CostEstimate(
            flops=4 * peers * CAP * G * peers * span * HD,
            bytes_accessed=32 * 2**20,
            transcendentals=peers * CAP * G * peers * span,
        ),
        name=name,
    )(*((q, kv) if begun is None else (q, kv, begun)))


def half_rows(rows, part):
    step = rows.shape[0] // 8
    half = step // 2
    return jnp.concatenate([rows[b * step + part * half : b * step + (part + 1) * half] for b in range(8)], axis=0)


def collect_kernel(col_ref, row_ref, replies_ref, low_ref, high_ref):
    slot = slots_as_col(col_ref[...], row_ref[...])
    n = slot.shape[0]
    pick = jnp.where(lax.broadcasted_iota(jnp.int32, (n, replies_ref.shape[0]), 1) == slot, 1.0, 0.0)
    rows = jnp.dot(pick.astype(BF16), replies_ref[...], preferred_element_type=F32).astype(BF16)
    low_ref[...] = half_rows(rows, 0)
    high_ref[...] = half_rows(rows, 1)


def collect(ids_col, ids_row, replies):
    n = ids_col.shape[0]
    return pl.pallas_call(
        collect_kernel,
        out_shape=(jax.ShapeDtypeStruct((n // 2, replies.shape[1]), BF16),) * 2,
        compiler_params=pltpu.CompilerParams(vmem_limit_bytes=32 * 2**20),
        cost_estimate=pl.CostEstimate(
            flops=2 * n * replies.shape[0] * replies.shape[1], bytes_accessed=2**21, transcendentals=0
        ),
        name="collect",
    )(ids_col, ids_row, replies)


def merge_kernel(part, me_ref, col_ref, row_ref, own_ref, far_ref, suf_ref, suf_lse_ref, w_ref, send_ref, keep_ref, att_ref, w_buf, sem):
    tile = w_ref.shape[1] // sem.shape[0]
    fetches = [
        pltpu.make_async_copy(
            w_ref.at[:, pl.ds(t * tile, tile)], w_buf.at[:, pl.ds(t * tile, tile)], sem.at[t]
        )
        for t in range(sem.shape[0])
    ]
    for fetch in fetches:
        fetch.start()
    n, width = suf_ref.shape
    slot = slots_as_col(col_ref[...], row_ref[...])
    pick = jnp.where(lax.broadcasted_iota(jnp.int32, (n, own_ref.shape[0]), 1) == slot, 1.0, 0.0)
    pick = half_rows(pick.astype(BF16), part)
    own = jnp.dot(pick, own_ref[...], preferred_element_type=F32)
    far = far_ref[...]
    i = lax.broadcasted_iota(jnp.int32, (HD, width), 0)
    c = lax.broadcasted_iota(jnp.int32, (HD, width), 1)
    spread = jnp.where((i < 24) & ((i & 7) == (c >> 7)), 1.0, 0.0).astype(BF16)
    own_lse = jnp.dot(own[:, width:].astype(BF16), spread, preferred_element_type=F32)
    far_lse = jnp.dot(far[:, width:], spread, preferred_element_type=F32)
    suf_lse = half_rows(suf_lse_ref, part)
    top = jnp.maximum(jnp.maximum(own_lse, far_lse), suf_lse)
    a = jnp.exp(own_lse - top)
    b = jnp.exp(far_lse - top)
    s = jnp.exp(suf_lse - top)
    att = a * own[:, :width] + b * far[:, :width].astype(F32) + s * half_rows(suf_ref, part)
    att_ref[0] = (att / (a + b + s)).astype(BF16)
    me = me_ref[0]
    step = att_ref.shape[1] // 8
    for q in range(8):
        flip = (1 - q // 4) + 2 * (1 - (q // 2) % 2) + 4 * (1 - q % 2)
        at = pl.multiple_of((me ^ flip) * step, step)
        att_ref[1, q * step : (q + 1) * step] = att_ref[0, pl.ds(at, step), :]
    half = send_ref.shape[0]
    for t, fetch in enumerate(fetches):
        fetch.wait()
        out = jnp.dot(
            att_ref[1], w_buf[:, t * tile : (t + 1) * tile], preferred_element_type=F32
        ).astype(BF16)
        send_ref[:, t * tile : (t + 1) * tile] = out[:half]
        keep_ref[:, t * tile : (t + 1) * tile] = out[half:]


def merge_project(part, me, ids_col, ids_row, own, far, suf, suf_lse, weight):
    n, width = suf.shape
    columns = weight.shape[1]
    whole = pl.BlockSpec(memory_space=pltpu.VMEM)
    shape = jax.ShapeDtypeStruct((n // 4, columns), BF16)
    return pl.pallas_call(
        functools.partial(merge_kernel, part),
        out_shape=(shape, shape),
        in_specs=[pl.BlockSpec(memory_space=pltpu.SMEM)]
        + [whole] * 6
        + [pl.BlockSpec(memory_space=pl.ANY)],
        out_specs=(whole, whole),
        scratch_shapes=[
            pltpu.VMEM((2, n // 2, width), BF16),
            pltpu.VMEM((width, columns), BF16),
            pltpu.SemaphoreType.DMA((8,)),
        ],
        compiler_params=pltpu.CompilerParams(vmem_limit_bytes=56 * 2**20),
        cost_estimate=pl.CostEstimate(
            flops=8 * n * width * columns, bytes_accessed=24 * 2**20, transcendentals=2 * n * width
        ),
        name="merge_project",
    )(me, ids_col, ids_row, own, far, suf, suf_lse, weight)


def suffix_attend(queries, suffix_cache, suffix_len):
    seq, width = queries.shape
    rows = suffix_cache.shape[1]
    heads = queries.reshape(seq, width // HD, HD)
    scores = (
        jnp.einsum("sgd,std->sgt", heads, suffix_cache[:, :, 0], preferred_element_type=F32) * SCALE
    )
    in_length = (jnp.arange(rows, dtype=jnp.int32)[None, :] < suffix_len[:, None])[:, None, :]
    scores = jnp.where(in_length, scores, LOW)
    highest = jnp.max(scores, axis=-1)
    exp_terms = jnp.where(in_length, jnp.exp(scores - highest[..., None]), 0.0)
    totals = jnp.sum(exp_terms, axis=-1)
    out = (
        jnp.einsum("sgt,std->sgd", exp_terms.astype(BF16), suffix_cache[:, :, 1], preferred_element_type=F32)
        / totals[..., None]
    )
    lse = jnp.broadcast_to((highest + jnp.log(totals))[..., None], out.shape)
    return out.reshape(seq, width), lse.reshape(seq, width)


def swap(value, axis, bit):
    size = lax.axis_size(axis)
    return lax.ppermute(value, axis, [(i, i ^ bit) for i in range(size)])


def local(prefill_pages, page_owner, queries, suffix_cache, suffix_len, prefix_id, out_weight):
    plane = lax.axis_size("x") * lax.axis_size("y")
    pages, page = prefill_pages.shape[:2]
    seq, width = queries.shape
    pairs = pages // 2
    ids_col, ids_row = prefix_id, prefix_id.reshape(1, seq)
    far_row = swap(ids_row, "zh", 1)

    sent = dispatch(ids_row, queries, plane * 2 * CAP).reshape(plane, 2 * CAP, width)
    own_q = lax.all_to_all(sent, PLANE, 0, 0, tiled=True)

    owner = page_owner[0, ::2]
    slot = slot_base(owner) // CAP
    here = jnp.arange(2 * plane, dtype=jnp.int32)[:, None] == slot[None, :]
    pick = jnp.sum(jnp.where(here, jnp.arange(pairs, dtype=jnp.int32)[None, :] + 1, 0), axis=1) - 1
    paired = jnp.swapaxes(prefill_pages.reshape(pairs, 2 * page, 2, HD), 1, 2)
    paired = paired.reshape(pairs, 4 * page, HD)
    first, second = place(pick, paired, plane)
    first, second, own_q, far_row = lax.optimization_barrier((first, second, own_q, far_row))
    far_col = far_row.reshape(seq, 1)
    far_q = swap(own_q, "zh", 1)
    first = lax.all_to_all(first, PLANE, 0, 0, tiled=True)
    first, second = lax.optimization_barrier((first, second))
    second = lax.all_to_all(second, PLANE, 0, 0, tiled=True)
    own_out = attend(own_q, first, "attend_own", 0)
    own_out, later, suffix_cache = lax.optimization_barrier((own_out, queries, suffix_cache))
    suf, suf_lse = suffix_attend(later, suffix_cache, suffix_len)
    far_q, own_out, suf, suf_lse = lax.optimization_barrier((far_q, own_out, suf, suf_lse))
    far_out = attend(far_q, first, "attend_far", 0)
    far_out = attend(far_q, second, "attend_far", 1, far_out)
    far_out, own_q = lax.optimization_barrier((far_out, own_q))
    far_back = lax.all_to_all(far_out, PLANE, 0, 0, tiled=True)
    own_out = attend(own_q, second, "attend_own", 1, own_out)
    far_back, own_out = lax.optimization_barrier((far_back, own_out))
    far_part = collect(far_col, far_row, far_back.reshape(plane * 2 * CAP, width + HD))
    far_part, own_out = lax.optimization_barrier((far_part, own_out))
    far_low = swap(far_part[0], "zh", 1)
    far_high = swap(far_part[1], "zh", 1)
    own_back = lax.all_to_all(own_out, PLANE, 0, 0, tiled=True)

    me = (lax.axis_index("zl") * 2 + lax.axis_index("core")).astype(jnp.int32).reshape(1)
    own_back = own_back.reshape(plane * 2 * CAP, width + HD)
    halves = [
        merge_project(part, me, ids_col, ids_row, own_back, far, suf, suf_lse, out_weight)
        for part, far in enumerate((far_low, far_high))
    ]

    def add(a, b):
        return (a.astype(F32) + b.astype(F32)).astype(BF16)

    got = [swap(send, "core", 1) for send, _ in halves]
    step = halves[0][1].shape[0] // 4

    def block(q):
        rows = slice(q * step, (q + 1) * step)
        return jnp.concatenate([add(keep[rows], g[rows]) for (_, keep), g in zip(halves, got)], axis=0)

    parts = [swap(block(q), "zl", bit) for q, bit in ((0, 3), (2, 2), (1, 1))]
    total = block(3).astype(F32)
    for part in parts:
        total = total + part.astype(F32)
    return total.astype(BF16)


def solution(mesh):
    x, zh, y, zl, core = 4, 2, 4, 4, 2
    names = ("x", "zh", "y", "zl", "core")
    fine = Mesh(mesh.devices.reshape(x, zh, y, zl, core), names)
    pool, tp = ("x", "zh", "y"), ("zl", "core")
    in_specs = (
        P(pool, None, None, tp),
        P(pool, None),
        P(pool, tp),
        P(pool, None, None, tp),
        P(pool),
        P(pool, None),
        P(tp, None),
    )
    out_specs = P(pool + tp, None)
    return jax.shard_map(local, mesh=fine, in_specs=in_specs, out_specs=out_specs, check_vma=False)
```
